256 devices in a mesh: dm: 4 (over x), fft: 64 (over y, z, core).
Axes of the slice: x: 4, y: 4, z: 8, core: 2. Of those that a mesh axis runs over, the one named last changes fastest.
Arguments:
- series: float32 [16777216], P(('dm', 'fft')), parts along dimension 0, may hold values from -6 to 6
- filters: float32 [32, 16], replicated, may hold values from -1.5 to 1.5
- delays: int32 [2, 1024], P(None, 'fft'), may hold values from -48 to 48, as said below
- phases: int32 [2, 1024], P(None, 'fft'), may hold values from 0 to 31
Outputs:
- harmonic_power: float32 [8, 64, 1024], P('dm', 'fft'), parts along dimension 0
The draws below stay inside these ranges and needn't reach their ends.
There are 4 independent parts, one for each index of `dm`. The reference program is written for one: setup_inputs(seed, part) draws one part's arguments, and reference() takes and returns one part's arrays. A program takes and returns all parts, laid end to end along the dimension named above; an argument that names none is the same for every part. Nothing has to cross between parts.
Inputs may be any that keep to these rules, and one draw needn't show every extreme that they name: `delays`: in every even row some trial's delay is -48, in every odd row some trial's delay is 48.
All inputs are finite; a program needn't handle non-finite values.
Results may differ from the reference program's by a relative error of at most 0.0001.
Values sent between devices are 32-bit elements; how exact they have to be, the bound alone decides.
A program may use at most 64 MiB of HBM per device.

```python
import jax
import jax.numpy as jnp
from jax import lax

ROWS = 1024
COLS = 4096
LENGTH = 4194304
TRIALS = 2
TAPS = 16
PHASES = 32
MAXD = 48
REACH = 56
HARMONICS = 8
FUND_DEV = 1024
N_FFT = 64


def draw_delays(key, part):
    key = jax.random.fold_in(key, 7)
    first, second = jax.random.split(key)
    values = jax.random.randint(first, (TRIALS, ROWS), -MAXD, MAXD + 1)
    chosen = jax.random.randint(second, (ROWS,), 0, TRIALS)
    rows = jnp.arange(ROWS, dtype=jnp.int32)
    edge = jnp.where(rows % 2 == 0, -MAXD, MAXD)
    pick = jnp.arange(TRIALS, dtype=jnp.int32)[:, None] == chosen[None, :]
    return jnp.where(pick, edge[None, :], values).astype(jnp.int32)


def plant(values, stream_key, least, high):
    extent = values.shape
    spot = [jax.random.randint(jax.random.fold_in(stream_key, axis), (), 0, extent[axis]) for axis in range(len(extent))]
    values = values.at[tuple(spot)].set(least)
    longest = extent.index(max(extent))
    spot[longest] = (spot[longest] + 1) % extent[longest]
    return values.at[tuple(spot)].set(high)


def shard_levels(stream_key, extent, pieces, least, high):
    loudness = 1.0
    for axis_at, parts in pieces:
        heights = jax.random.uniform(jax.random.fold_in(jax.random.fold_in(stream_key, 6), axis_at), (parts,), jnp.float32, least / len(pieces), high / len(pieces))
        loudness = loudness * jnp.repeat(jnp.exp(heights), extent[axis_at] // parts).reshape((-1,) + (1,) * (len(extent) - 1 - axis_at))
    return loudness


def scatter_about(own_key, shape, scale, most, shards=(), held_as=jnp.bfloat16):
    loudness = shard_levels(own_key, shape, shards, -0.22, 0.18) if shards else 1.0
    result = jax.random.normal(own_key, shape, jnp.float32) * scale * loudness
    return jnp.minimum(jnp.maximum(result, -most), most).astype(held_as)


def setup_inputs(seed: int = 0, part: int = 0) -> dict:
    seeds = jax.random.split(jax.random.key(seed), 5)
    own_keys = jax.random.split(jax.random.fold_in(seeds[4], part), 5)
    series = scatter_about(own_keys[0], (LENGTH,), 1.0, 6.0, ((0, 64),), jnp.float32)
    filters = scatter_about(seeds[1], (PHASES, TAPS), TAPS ** -0.5, 1.5, (), jnp.float32)
    delays = draw_delays(jax.random.fold_in(seeds[4], 71), part)
    phases = plant(jax.random.randint(seeds[3], (TRIALS, ROWS), 0, PHASES), jax.random.fold_in(seeds[3], 1), 0, PHASES - 1).astype(jnp.int32)
    return dict(series=series, filters=filters, delays=delays, phases=phases)


def taps_sum(window, taps, width):
    total = taps[..., 0:1] * window[..., 0:width]
    for step in range(1, taps.shape[-1]):
        total = total + taps[..., step:step + 1] * window[..., step:step + width]
    return total


def reference(series, filters, delays, phases):
    padded = jnp.pad(series, (REACH, REACH))
    count = FUND_DEV * N_FFT
    outputs = []
    for trial in range(TRIALS):
        starts = REACH + jnp.arange(ROWS, dtype=jnp.int32) * COLS + delays[trial].astype(jnp.int32) - TAPS // 2
        windows = jax.vmap(lambda begin: lax.dynamic_slice_in_dim(padded, begin, COLS + TAPS - 1))(starts)
        taps = filters[phases[trial]]
        resampled = taps_sum(windows, taps, COLS).reshape(ROWS * COLS)
        spectrum = jnp.fft.fft(resampled)
        power = (jnp.real(spectrum) ** 2 + jnp.imag(spectrum) ** 2) / (ROWS * COLS)
        total = power[0:count]
        for multiple in range(2, HARMONICS + 1):
            total = total + power[0:multiple * count:multiple]
        outputs.append((total / HARMONICS).reshape(FUND_DEV, N_FFT).T)
    return jnp.stack(outputs)
```

```python
import jax
import jax.numpy as jnp
import ml_dtypes
import numpy as np
from jax import lax
from jax.experimental import pallas as pl
from jax.experimental.pallas import tpu as pltpu
from jax.sharding import PartitionSpec as P

LENGTH = 4194304
SLOTS = 64
TAPS = 16
PHASES = 32
FIRST = 512
SECOND = 128
FREQS = 272
INVERSE = {1: 1, 3: 171, 5: 205, 7: 439}
BASES = {1: 0, 3: 16, 5: 32, 7: 48, 2: 64, 6: 96, 4: 128, 8: 144}
TERM_ROWS = 160


def split_table(table):
    table = np.asarray(table, np.float32)
    high = table.astype(ml_dtypes.bfloat16)
    low = (table - high.astype(np.float32)).astype(ml_dtypes.bfloat16)
    return high, low


def make_tables():
    turn = 2.0 * np.pi
    angle = turn / FIRST * (np.arange(FREQS)[:, None] * np.arange(FIRST)[None, :] % FIRST)
    first = np.concatenate([np.cos(angle), -np.sin(angle)], axis=0)
    h, a, rr, c_hi = np.meshgrid(
        np.arange(2), np.arange(2), np.arange(2), np.arange(32), indexing="ij"
    )
    second_index = (64 * rr + 2 * c_hi + h).reshape(-1)
    trial = a.reshape(-1)
    angle = turn / 65536 * (np.arange(FREQS)[:, None] * second_index[None, :] % 65536)
    mid = np.stack([np.cos(angle), -np.sin(angle)]).astype(np.float32)
    angle = turn / SECOND * (second_index[:, None] * np.arange(SECOND)[None, :] % SECOND)
    cos_part, sin_part = np.cos(angle), np.sin(angle)
    second = np.zeros((2, 256, 2, 2, SECOND))
    for t in range(2):
        own = (trial == t)[:, None]
        second[0, :, 0, t] = cos_part * own
        second[1, :, 0, t] = sin_part * own
        second[0, :, 1, t] = -sin_part * own
        second[1, :, 1, t] = cos_part * own
    second = second.reshape(512, 512)
    angle = turn / LENGTH * (np.arange(FREQS)[:, None] * np.arange(128)[None, :])
    col = np.stack([np.cos(angle), -np.sin(angle)]).astype(np.float32)
    angle = turn / 8192 * (np.arange(SLOTS)[:, None] * np.arange(SECOND)[None, :] % 8192)
    row = np.stack([np.cos(angle), -np.sin(angle)]).astype(np.float32)
    last = np.zeros((2, 2, 8, 4, 2, SLOTS, 4, 2, 2))
    special = np.zeros((2, 2, 2, 8, SLOTS, 4, 2, 2))
    q = np.arange(SLOTS)
    for sign in range(2):
        for p in range(8):
            actual = p if sign == 0 else -1 - p
            theta = turn / 64 * (q * actual % 64)
            for i in range(4):
                for t in range(2):
                    last[0, sign, p, i, t, :, i, 0, t] = np.cos(theta)
                    last[0, sign, p, i, t, :, i, 1, t] = np.sin(theta)
                    last[1, sign, p, i, t, :, i, 0, t] = -np.sin(theta)
                    last[1, sign, p, i, t, :, i, 1, t] = np.cos(theta)
            theta = turn / 128 * (q * (2 * p + sign) % 128)
            for t in range(2):
                special[0, sign, t, p, :, 0, sign, t] = np.cos(theta)
                special[1, sign, t, p, :, 0, sign, t] = -np.sin(theta)
    last = np.concatenate([last.reshape(256, 1024), special.reshape(64, 1024)], axis=0)
    return (*split_table(first), *split_table(second), *split_table(last), mid, col, row)


def split(x):
    high = x.astype(jnp.bfloat16)
    return high, (x - high.astype(jnp.float32)).astype(jnp.bfloat16)


def product(a_high, a_low, b_high, b_low):
    def dot(a, b):
        return jnp.dot(a, b, preferred_element_type=jnp.float32)

    return dot(a_high, b_high) + dot(a_low, b_high) + dot(a_high, b_low)


def lanes_at(x, index):
    return jnp.take_along_axis(x, index, axis=1, mode="promise_in_bounds")


def iota(shape, axis):
    return lax.broadcasted_iota(jnp.int32, shape, axis)


def column_of(values, own, second_trial):
    chosen = jnp.where(second_trial, values[1:2, :], values[0:1, :])
    return jnp.sum(jnp.where(own, chosen, 0.0), axis=1, keepdims=True)


def kernel(
    series, delays, phases, filters,
    first_high, first_low, second_high, second_low, last_high, last_low, mid, col, row,
    out,
    ext, responses, send1, recv1, send2, recv2, powers, rows_a, terms, received,
    v_first_high, v_first_low, v_second_high, v_second_low, v_last_high, v_last_low,
    v_mid, v_col, v_row, spectrum,
    table_sem, series_sem, halo_send, halo_recv,
    send1_sem, recv1_sem, send2_sem, recv2_sem, term_send, term_recv,
):
    me = lax.axis_index("fft")
    f32 = jnp.float32

    barrier = pltpu.get_barrier_semaphore()

    def greet(step, carry):
        pl.semaphore_signal(
            barrier, inc=1, device_id={"fft": (me + step) & (SLOTS - 1)},
            device_id_type=pl.DeviceIdType.MESH,
        )
        return carry

    lax.fori_loop(1, SLOTS, greet, 0)

    own_series = pltpu.make_async_copy(series, ext.at[pl.ds(8, 512)], series_sem)
    own_series.start()
    tables = [
        pltpu.make_async_copy(source, target, table_sem.at[n])
        for n, (source, target) in enumerate(
            (
                (first_high, v_first_high), (first_low, v_first_low),
                (second_high, v_second_high), (second_low, v_second_low),
                (last_high, v_last_high), (last_low, v_last_low),
                (mid, v_mid), (col, v_col), (row, v_row),
            )
        )
    ]
    for copy in tables:
        copy.start()

    line = iota((32, 16), 0)
    own = iota((32, 16), 1) == 2 * (line >> 2) + (line & 1)
    second_trial = ((line >> 1) & 1) == 1
    delay = column_of(delays[...].astype(f32), own, second_trial)
    phase = column_of(phases[...].astype(f32), own, second_trial)
    taps = jnp.zeros((32, TAPS), f32)
    for branch in range(PHASES):
        taps = jnp.where(phase == float(branch), filters[branch : branch + 1, :], taps)
    position = iota((32, 256), 1).astype(f32)
    response = jnp.zeros((32, 256), f32)
    for tap in range(TAPS):
        response = jnp.where(position == delay + (56.0 + tap), taps[:, tap : tap + 1], response)
    responses[...] = response

    pl.semaphore_wait(barrier, SLOTS - 1)

    @pl.when(me == 0)
    def _():
        ext[0:8, :] = jnp.zeros((8, 128), f32)

    @pl.when(me == SLOTS - 1)
    def _():
        ext[520:528, :] = jnp.zeros((8, 128), f32)

    to_next = pltpu.make_async_remote_copy(
        src_ref=series.at[pl.ds(504, 8)], dst_ref=ext.at[pl.ds(0, 8)],
        send_sem=halo_send.at[0], recv_sem=halo_recv.at[0],
        device_id={"fft": (me + 1) & (SLOTS - 1)}, device_id_type=pl.DeviceIdType.MESH,
    )
    to_last = pltpu.make_async_remote_copy(
        src_ref=series.at[pl.ds(0, 8)], dst_ref=ext.at[pl.ds(520, 8)],
        send_sem=halo_send.at[1], recv_sem=halo_recv.at[1],
        device_id={"fft": (me + SLOTS - 1) & (SLOTS - 1)}, device_id_type=pl.DeviceIdType.MESH,
    )

    @pl.when(me < SLOTS - 1)
    def _():
        to_next.start()

    @pl.when(me > 0)
    def _():
        to_last.start()

    own_series.wait()

    @pl.when(me > 0)
    def _():
        to_next.wait_recv()

    @pl.when(me < SLOTS - 1)
    def _():
        to_last.wait_recv()

    lane = iota((64, 128), 1)
    block_of = iota((128, 128), 1) >> 5

    def resample(rg, carry):
        before = ext[pl.ds(64 * rg + 7, 64), :]
        here = ext[pl.ds(pl.multiple_of(64 * rg + 8, 8), 64), :]
        after = ext[pl.ds(64 * rg + 9, 64), :]
        left = pltpu.roll(jnp.where(lane < 64, here, before), 64, 1)
        right = pltpu.roll(jnp.where(lane < 64, after, here), 64, 1)
        window = jnp.concatenate(
            [jnp.concatenate([left, left], 0).T, jnp.concatenate([right, right], 0).T], 0
        )
        w_high, w_low = split(window)
        total = jnp.zeros((128, 128), f32)
        for block in range(4):
            line = responses[pl.ds(4 * rg + block, 1), :]
            band = pltpu.roll(jnp.broadcast_to(line, (128, 256)), 0, 1, stride=1, stride_axis=0)
            b_high, b_low = split(band)
            total = jnp.where(block_of == block, product(b_high, b_low, w_high, w_low), total)
        send1[pl.ds(rg, 64, stride=16), :] = total[0:64]
        send1[pl.ds(8 + rg, 64, stride=16), :] = total[64:128]
        return carry

    lax.fori_loop(0, 8, resample, 0)

    def exchange(source, target, send_sem, recv_sem):
        mine = pl.ds(pl.multiple_of(16 * me, 16), 16)

        def send(step, carry):
            to = (me + step) & (SLOTS - 1)
            pltpu.make_async_remote_copy(
                src_ref=source.at[pl.ds(pl.multiple_of(16 * to, 16), 16)],
                dst_ref=target.at[mine],
                send_sem=send_sem, recv_sem=recv_sem,
                device_id={"fft": to}, device_id_type=pl.DeviceIdType.MESH,
            ).start()
            return carry

        lax.fori_loop(1, SLOTS, send, 0)
        pltpu.make_async_copy(source.at[mine], target.at[mine], recv_sem).start()

    def arrived(target, sem):
        pltpu.make_async_copy(target, target, sem).wait()

    def sent(source, sem):
        part = source.at[pl.ds(0, 16 * (SLOTS - 1))]
        pltpu.make_async_copy(part, part, sem).wait()

    exchange(send1, recv1, send1_sem, recv1_sem)
    for copy in tables:
        copy.wait()
    me_lane = iota((FREQS, 128), 1) == me
    col_cos = jnp.sum(jnp.where(me_lane, v_col[0], 0.0), axis=1, keepdims=True)
    col_sin = jnp.sum(jnp.where(me_lane, v_col[1], 0.0), axis=1, keepdims=True)
    row_cos = v_row[0, pl.ds(me, 1), :]
    row_sin = v_row[1, pl.ds(me, 1), :]
    turn_cos = col_cos * row_cos - col_sin * row_sin
    turn_sin = col_cos * row_sin + col_sin * row_cos
    arrived(recv1, recv1_sem)

    block = recv1[...].reshape(SLOTS, 2, 8, 128)
    data = jnp.concatenate(
        [block[:, 0].reshape(FIRST, 128), block[:, 1].reshape(FIRST, 128)], 1
    )
    d_high, d_low = split(data)
    spectrum[...] = product(v_first_high[...], v_first_low[...], d_high, d_low)
    real, imaginary = spectrum[0:FREQS, :], spectrum[FREQS : 2 * FREQS, :]
    mid_cos, mid_sin = v_mid[0], v_mid[1]
    turned = jnp.concatenate(
        [real * mid_cos - imaginary * mid_sin, real * mid_sin + imaginary * mid_cos], 1
    )
    t_high, t_low = split(turned)
    result = product(t_high, t_low, v_second_high[...], v_second_low[...])
    lane1 = iota((1, 128), 1)
    for t in range(2):
        real = result[:, 128 * t : 128 * t + 128]
        imaginary = result[:, 256 + 128 * t : 384 + 128 * t]
        parts = (
            real * turn_cos - imaginary * turn_sin,
            real * turn_sin + imaginary * turn_cos,
        )
        middle = pltpu.roll(real[0:1], 64, 1)
        for c in range(2):
            for i in range(4):
                send2[pl.ds(4 * i + 2 * c + t, 64, stride=16), :] = parts[c][64 * i : 64 * i + 64]
            packed = jnp.where(lane1 < 64, parts[c][0:1], pltpu.roll(parts[c][256:257], 64, 1))
            if c == 1:
                packed = jnp.where(lane1 == 0, middle, packed)
            send2[2 * c + t : 2 * c + t + 1, :] = packed

    exchange(send2, recv2, send2_sem, recv2_sem)
    arrived(recv2, recv2_sem)

    r_high, r_low = split(recv2[...])
    final = product(v_last_high[...], v_last_low[...], r_high, r_low)
    power = final[0:128] ** 2 + final[128:256] ** 2
    special = final[256:288] ** 2 + final[288:320] ** 2
    powers[...] = power
    lane8, sub8 = iota((8, 128), 1), iota((8, 128), 0)

    @pl.when(me == 0)
    def _():
        for sign in range(2):
            for t in range(2):
                where = pl.ds(64 * sign + t, 8, stride=8)
                at = 16 * sign + 8 * t
                powers[where, :] = jnp.where(lane8 == 0, special[at : at + 8], powers[where, :])
        for p in range(8):
            plus = powers[8 * p : 8 * p + 8, :]
            minus = powers[64 + 8 * p : 72 + 8 * p, :]
            head = sub8 < 2
            powers[8 * p : 8 * p + 8, :] = jnp.where(
                head & (lane8 >= 64), lanes_at(minus, (128 - lane8) & 63), plus
            )
            index = jnp.where(head, 191 - lane8, 127 - lane8) & 127
            turned = jnp.where(
                head & (lane8 < 64), lanes_at(plus, (lane8 + 64) & 127), lanes_at(minus, index)
            )
            powers[64 + 8 * p : 72 + 8 * p, :] = pltpu.roll(turned, 6, 0)

    @pl.when(me != 0)
    def _():
        for p in range(8):
            minus = powers[64 + 8 * p : 72 + 8 * p, :]
            powers[64 + 8 * p : 72 + 8 * p, :] = lanes_at(minus, 127 - lane8)

    for sign in range(2):
        for i in range(4):
            for t in range(2):
                rows_a[pl.ds(64 * sign + 16 * i + t, 8, stride=2), :] = powers[
                    pl.ds(64 * sign + 2 * i + t, 8, stride=8), :
                ]

    def residue(sign):
        return me if sign == 0 else (SLOTS - me) & (SLOTS - 1)

    def select(sign, m, odd, share, half):
        slot = sub8 >> 1
        place = slot if sign == 0 else 7 - slot
        k1 = (INVERSE[odd] * ((residue(sign) + 64 * place) // share)) & (FIRST // share - 1)
        index = ((m * k1) >> 9) + odd * (128 * half + lane8)
        total = jnp.zeros((8, 128), f32)
        for p in range(odd * half, odd * half + odd):
            at = 64 * sign + 8 * p
            total = jnp.where(
                (index >> 7) == p, lanes_at(powers[at : at + 8, :], index & 127), total
            )
        return total

    started = []

    def give(source, start, m, sign, rows, to, condition):
        base = BASES[m] + (0 if m == 8 else rows * sign)
        from_ref = source.at[pl.ds(start, rows)]
        to_ref = received.at[pl.ds(base, rows)]
        number = len(started)
        copy = pltpu.make_async_remote_copy(
            src_ref=from_ref, dst_ref=to_ref,
            send_sem=term_send.at[number], recv_sem=term_recv,
            device_id={"fft": to}, device_id_type=pl.DeviceIdType.MESH,
        )
        away = condition & (to != me)

        @pl.when(away)
        def _():
            copy.start()

        @pl.when(condition & (to == me))
        def _():
            pltpu.make_async_copy(from_ref, to_ref, term_recv).start()

        started.append((copy, away))

    for sign in range(2):
        rest = residue(sign)
        always = me >= 0
        even = (me & 1) == 0
        give(powers, 64 * sign, 1, sign, 8, rest, always)
        for v in range(2):
            give(powers, 64 * sign, 2, sign, 16, ((rest >> 1) + 32 * v) & 63, even)
        for i in range(4):
            place = i if sign == 0 else 7 - i
            give(rows_a, 64 * sign + 16 * i, 4, sign, 8, ((rest >> 2) + 16 * place) & 63, (me & 3) == 0)
            give(rows_a, 64 * sign + 16 * i, 8, sign, 16, ((rest >> 3) + 8 * place) & 63, (me & 7) == 0)
    for n, m in enumerate((3, 5, 7)):
        for sign in range(2):
            at = 16 * n + 8 * sign
            terms[at : at + 8, :] = select(sign, m, m, 1, 0)
            give(terms, at, m, sign, 8, (INVERSE[m] * residue(sign)) & 63, me >= 0)
    for sign in range(2):
        for half in range(2):
            at = 48 + 16 * sign + 8 * half
            terms[at : at + 8, :] = select(sign, 6, 3, 2, half)
        for v in range(2):
            to = (INVERSE[3] * ((residue(sign) >> 1) + 32 * v)) & 63
            give(terms, 48 + 16 * sign, 6, sign, 16, to, (me & 1) == 0)

    arrived(received, term_recv)

    def source_row(m, v, rows):
        place = (((m * me) >> 6) + m * v) & 7
        sign = place >> 2
        slot = jnp.where(sign == 1, 7 - place, place)
        return BASES[m] + rows * sign + 2 * slot

    for t in range(2):
        total = received[pl.ds(BASES[8] + t, 8, stride=2), :]
        for v in range(2):
            base = BASES[4] + 8 * v + t
            values = jnp.broadcast_to(received[base : base + 1, :], (8, 128))
            for p in range(1, 4):
                values = jnp.where((sub8 >> 1) == p, received[base + 2 * p : base + 2 * p + 1, :], values)
            values = lanes_at(values, 64 * (sub8 & 1) + (lane8 >> 1))
            total = total + jnp.where((lane8 & 1) == v, values, 0.0)
        for v in range(4):
            at2 = source_row(2, v, 16) + t
            at6 = source_row(6, v, 16) + t
            low = received[pl.ds(at2, 1), :] + received[pl.ds(at6, 1), :]
            high = received[pl.ds(at2 + 8, 1), :] + received[pl.ds(at6 + 8, 1), :]
            values = jnp.where((sub8 >> 2) == 0, low, high)
            values = lanes_at(values, 32 * (sub8 & 3) + (lane8 >> 2))
            total = total + jnp.where((lane8 & 3) == v, values, 0.0)
        for v in range(8):
            values = received[pl.ds(source_row(1, v, 8) + t, 1), :]
            for m in (3, 5, 7):
                values = values + received[pl.ds(source_row(m, v, 8) + t, 1), :]
            values = lanes_at(jnp.broadcast_to(values, (8, 128)), 16 * sub8 + (lane8 >> 3))
            total = total + jnp.where((lane8 & 7) == v, values, 0.0)
        out[t] = total * (0.125 / LENGTH)

    @pl.when(me < SLOTS - 1)
    def _():
        to_next.wait_send()

    @pl.when(me > 0)
    def _():
        to_last.wait_send()

    sent(send1, send1_sem)
    sent(send2, send2_sem)
    for copy, away in started:

        @pl.when(away)
        def _(copy=copy):
            copy.wait_send()


def on_device(series, filters, delays, phases):
    tables = [jnp.asarray(table) for table in make_tables()]
    whole = pl.BlockSpec(memory_space=pltpu.VMEM)
    anywhere = pl.BlockSpec(memory_space=pl.ANY)
    f32 = jnp.float32
    out = pl.pallas_call(
        kernel,
        out_shape=jax.ShapeDtypeStruct((2, 8, 128), f32),
        in_specs=[anywhere, whole, whole, whole] + [anywhere] * len(tables),
        out_specs=whole,
        scratch_shapes=[
            pltpu.VMEM((528, 128), f32),
            pltpu.VMEM((32, 256), f32),
            pltpu.VMEM((1024, 128), f32),
            pltpu.VMEM((1024, 128), f32),
            pltpu.VMEM((1024, 128), f32),
            pltpu.VMEM((1024, 128), f32),
            pltpu.VMEM((128, 128), f32),
            pltpu.VMEM((128, 128), f32),
            pltpu.VMEM((80, 128), f32),
            pltpu.VMEM((TERM_ROWS, 128), f32),
        ]
        + [pltpu.VMEM(table.shape, table.dtype) for table in tables]
        + [
            pltpu.VMEM((2 * FREQS, 256), f32),
            pltpu.SemaphoreType.DMA((len(tables),)),
            pltpu.SemaphoreType.DMA,
            pltpu.SemaphoreType.DMA((2,)),
            pltpu.SemaphoreType.DMA((2,)),
            pltpu.SemaphoreType.DMA,
            pltpu.SemaphoreType.DMA,
            pltpu.SemaphoreType.DMA,
            pltpu.SemaphoreType.DMA,
            pltpu.SemaphoreType.DMA((32,)),
            pltpu.SemaphoreType.DMA,
        ],
        compiler_params=pltpu.CompilerParams(
            collective_id=0, has_side_effects=True, vmem_limit_bytes=48 * 1024 * 1024
        ),
    )(series.reshape(512, 128), delays, phases, filters, *tables)
    return out.reshape(2, 1, 1024)


def solution(mesh):
    return jax.shard_map(
        on_device,
        mesh=mesh,
        in_specs=(P(("dm", "fft")), P(), P(None, "fft"), P(None, "fft")),
        out_specs=P("dm", "fft", None),
        check_vma=False,
    )
```

```python
import jax
import jax.numpy as jnp
import ml_dtypes
import numpy as np
from jax import lax
from jax.experimental import pallas as pl
from jax.experimental.pallas import tpu as pltpu
from jax.sharding import PartitionSpec as P

LENGTH = 4194304
SLOTS = 64
TAPS = 16
PHASES = 32
FIRST = 512
SECOND = 128
FREQS = 272
INVERSE = {1: 1, 3: 171, 5: 205, 7: 439}
BASES = {1: 0, 3: 16, 5: 32, 7: 48, 2: 64, 6: 96, 4: 128, 8: 144}
TERM_ROWS = 152


def split_table(table):
    table = np.asarray(table, np.float32)
    high = table.astype(ml_dtypes.bfloat16)
    low = (table - high.astype(np.float32)).astype(ml_dtypes.bfloat16)
    return high, low


def make_tables():
    turn = 2.0 * np.pi
    angle = turn / FIRST * (np.arange(FREQS)[:, None] * np.arange(FIRST)[None, :] % FIRST)
    first = np.concatenate([np.cos(angle), -np.sin(angle)], axis=0)
    h, rr, c_hi = np.meshgrid(np.arange(2), np.arange(2), np.arange(32), indexing="ij")
    second_index = (64 * rr + 2 * c_hi + h).reshape(-1)
    angle = turn / 65536 * (np.arange(FREQS)[:, None] * second_index[None, :] % 65536)
    mid = np.stack([np.cos(angle), -np.sin(angle)]).astype(np.float32)
    angle = turn / SECOND * (second_index[:, None] * np.arange(SECOND)[None, :] % SECOND)
    cos_part, sin_part = np.cos(angle), np.sin(angle)
    second = np.block([[cos_part, -sin_part], [sin_part, cos_part]])
    angle = turn / LENGTH * (np.arange(FREQS)[:, None] * np.arange(128)[None, :])
    col = np.stack([np.cos(angle), -np.sin(angle)]).astype(np.float32)
    angle = turn / 8192 * (np.arange(SLOTS)[:, None] * np.arange(SECOND)[None, :] % 8192)
    row = np.stack([np.cos(angle), -np.sin(angle)]).astype(np.float32)
    last = np.zeros((2, 8, 2, 4, SLOTS, 4, 2))
    special = np.zeros((2, 2, 8, SLOTS, 4, 2))
    q = np.arange(SLOTS)
    for sign in range(2):
        for p in range(8):
            actual = p if sign == 0 else -1 - p
            theta = turn / 64 * (q * actual % 64)
            for i in range(4):
                last[0, p, sign, i, :, i, 0] = np.cos(theta)
                last[0, p, sign, i, :, i, 1] = np.sin(theta)
                last[1, p, sign, i, :, i, 0] = -np.sin(theta)
                last[1, p, sign, i, :, i, 1] = np.cos(theta)
            theta = turn / 128 * (q * (2 * p + sign) % 128)
            special[0, sign, p, :, 0, sign] = np.cos(theta)
            special[1, sign, p, :, 0, sign] = -np.sin(theta)
    last = np.concatenate([last.reshape(128, 512), special.reshape(32, 512)], axis=0)
    return (*split_table(first), *split_table(second), *split_table(last), mid, col, row)


def split(x):
    high = x.astype(jnp.bfloat16)
    return high, (x - high.astype(jnp.float32)).astype(jnp.bfloat16)


def dot(a, b):
    return jnp.dot(a, b, preferred_element_type=jnp.float32)


def product(a_high, a_low, b_high, b_low):
    wide = dot(a_high, jnp.concatenate([b_high, b_low], 1))
    return wide[:, 0:128] + wide[:, 128:256] + dot(a_low, b_high)


def lanes_at(x, index):
    return jnp.take_along_axis(x, index, axis=1, mode="promise_in_bounds")


def iota(shape, axis):
    return lax.broadcasted_iota(jnp.int32, shape, axis)


def column_of(values, own, second_trial):
    chosen = jnp.where(second_trial, values[1:2, :], values[0:1, :])
    return jnp.sum(jnp.where(own, chosen, 0.0), axis=1, keepdims=True)


def kernel(
    series, delays, phases, filters,
    first_high, first_low, second_high, second_low, last_high, last_low, mid, col, row,
    out,
    ext, responses, windows_high, windows_low, send1, recv1, send2, recv2, spectrum, turn,
    powers, rows_a, terms, received,
    v_first_high, v_first_low, v_second_high, v_second_low, v_last_high, v_last_low,
    v_mid, v_col, v_row,
    table_sem, series_sem, halo_send, halo_recv,
    send1_sem, recv1_sem, send2_sem, recv2_sem, term_send, term_recv,
):
    me = lax.axis_index("fft")
    f32 = jnp.float32
    mesh_id = pl.DeviceIdType.MESH

    barrier = pltpu.get_barrier_semaphore()

    def greet(step, carry):
        pl.semaphore_signal(
            barrier, inc=1, device_id={"fft": (me + step) & (SLOTS - 1)}, device_id_type=mesh_id
        )
        return carry

    lax.fori_loop(1, SLOTS, greet, 0)

    own_series = pltpu.make_async_copy(series, ext.at[pl.ds(8, 512)], series_sem)
    own_series.start()
    tables = [
        pltpu.make_async_copy(source, target, table_sem.at[n])
        for n, (source, target) in enumerate(
            (
                (first_high, v_first_high), (first_low, v_first_low),
                (second_high, v_second_high), (second_low, v_second_low),
                (last_high, v_last_high), (last_low, v_last_low),
                (mid, v_mid), (col, v_col), (row, v_row),
            )
        )
    ]
    for copy in tables:
        copy.start()

    line = iota((32, 16), 0)
    own = iota((32, 16), 1) == 2 * (line >> 2) + (line & 1)
    second_trial = ((line >> 1) & 1) == 1
    delay = column_of(delays[...].astype(f32), own, second_trial)
    phase = column_of(phases[...].astype(f32), own, second_trial)
    branch = (iota((32, PHASES), 1).astype(f32) == phase).astype(f32)
    taps = lax.dot_general(
        branch, filters[...], (((1,), (1,)), ((), ())),
        precision=lax.Precision.HIGHEST, preferred_element_type=f32,
    )
    position = iota((32, 256), 1).astype(f32) - (delay + 56.0)
    response = jnp.zeros((32, 256), f32)
    for tap in range(TAPS):
        response = jnp.where(position == float(tap), taps[:, tap : tap + 1], response)
    responses[...] = response

    pl.semaphore_wait(barrier, SLOTS - 1)
    to_next = pltpu.make_async_remote_copy(
        src_ref=series.at[pl.ds(504, 8)], dst_ref=ext.at[pl.ds(0, 8)],
        send_sem=halo_send.at[0], recv_sem=halo_recv.at[0],
        device_id={"fft": (me + 1) & (SLOTS - 1)}, device_id_type=mesh_id,
    )
    to_last = pltpu.make_async_remote_copy(
        src_ref=series.at[pl.ds(0, 8)], dst_ref=ext.at[pl.ds(520, 8)],
        send_sem=halo_send.at[1], recv_sem=halo_recv.at[1],
        device_id={"fft": (me + SLOTS - 1) & (SLOTS - 1)}, device_id_type=mesh_id,
    )

    @pl.when(me < SLOTS - 1)
    def _():
        to_next.start()

    @pl.when(me > 0)
    def _():
        to_last.start()

    own_series.wait()

    lane64 = iota((64, 128), 1)
    quarter = lane64 >> 5

    def resample(trial, rg):
        if trial == 0:
            before = ext[pl.ds(64 * rg + 7, 64), :]
            here = ext[pl.ds(64 * rg + 8, 64), :]
            after = ext[pl.ds(64 * rg + 9, 64), :]
            left = pltpu.roll(jnp.where(lane64 < 64, here, before), 64, 1)
            right = pltpu.roll(jnp.where(lane64 < 64, after, here), 64, 1)
            window = jnp.concatenate(
                [jnp.concatenate([left, left], 0).T, jnp.concatenate([right, right], 0).T], 0
            )
            w_high, w_low = split(window)
            windows_high[rg], windows_low[rg] = w_high, w_low
        else:
            w_high, w_low = windows_high[rg], windows_low[rg]
        bands = []
        for rr in range(2):
            line = responses[pl.ds(4 * rg + 2 * trial + rr, 1), :]
            bands.append(
                pltpu.roll(jnp.broadcast_to(line, (128, 256)), 0, 1, stride=1, stride_axis=0)
            )
        b_high, b_low = split(jnp.concatenate(bands, 0))
        both = product(b_high, b_low, w_high, w_low)
        total = jnp.where((quarter & 1) == 0, both[0:64], both[128:192])
        later = jnp.where((quarter & 1) == 0, both[64:128], both[192:256])
        send1[trial, pl.ds(rg, 64, stride=8), :] = jnp.where(quarter < 2, total, later)

    def exchange(source, target, send_sem, recv_sem):
        mine = pl.ds(pl.multiple_of(8 * me, 8), 8)

        def send(step, carry):
            to = (me + step) & (SLOTS - 1)
            pltpu.make_async_remote_copy(
                src_ref=source.at[pl.ds(pl.multiple_of(8 * to, 8), 8)],
                dst_ref=target.at[mine],
                send_sem=send_sem, recv_sem=recv_sem,
                device_id={"fft": to}, device_id_type=mesh_id,
            ).start()
            return carry

        lax.fori_loop(1, SLOTS, send, 0)
        pltpu.make_async_copy(source.at[mine], target.at[mine], recv_sem).start()

    def arrived(target, sem):
        pltpu.make_async_copy(target, target, sem).wait()

    def sent(source, sem):
        part = source.at[pl.ds(0, 8 * (SLOTS - 1))]
        pltpu.make_async_copy(part, part, sem).wait()

    def inner(trial):
        def body(rg, carry):
            resample(trial, rg)
            return carry

        return body

    lax.fori_loop(1, 7, inner(0), 0)

    @pl.when(me > 0)
    def _():
        to_next.wait_recv()

    @pl.when(me == 0)
    def _():
        ext[0:8, :] = jnp.zeros((8, 128), f32)

    @pl.when(me < SLOTS - 1)
    def _():
        to_last.wait_recv()

    @pl.when(me == SLOTS - 1)
    def _():
        ext[520:528, :] = jnp.zeros((8, 128), f32)

    resample(0, 0)
    resample(0, 7)
    exchange(send1.at[0], recv1.at[0], send1_sem.at[0], recv1_sem.at[0])
    lax.fori_loop(0, 8, inner(1), 0)
    exchange(send1.at[1], recv1.at[1], send1_sem.at[1], recv1_sem.at[1])

    for copy in tables:
        copy.wait()
    me_lane = iota((FREQS, 128), 1) == me
    col_cos = jnp.sum(jnp.where(me_lane, v_col[0], 0.0), axis=1, keepdims=True)
    col_sin = jnp.sum(jnp.where(me_lane, v_col[1], 0.0), axis=1, keepdims=True)
    row_cos = v_row[0, pl.ds(me, 1), :]
    row_sin = v_row[1, pl.ds(me, 1), :]
    turn[0] = col_cos * row_cos - col_sin * row_sin
    turn[1] = col_cos * row_sin + col_sin * row_cos
    lane1 = iota((1, 128), 1)
    lane8, sub8 = iota((8, 128), 1), iota((8, 128), 0)

    def transform(trial):
        d_high, d_low = split(recv1[trial])
        spectrum[...] = product(v_first_high[...], v_first_low[...], d_high, d_low)
        real, imaginary = spectrum[0:FREQS, :], spectrum[FREQS : 2 * FREQS, :]
        mid_cos, mid_sin = v_mid[0], v_mid[1]
        turned = jnp.concatenate(
            [real * mid_cos - imaginary * mid_sin, real * mid_sin + imaginary * mid_cos], 1
        )
        t_high, t_low = split(turned)
        s_high = v_second_high[...]
        result = dot(t_high, s_high) + dot(t_low, s_high) + dot(t_high, v_second_low[...])
        real, imaginary = result[:, 0:128], result[:, 128:256]
        turn_cos, turn_sin = turn[0], turn[1]
        parts = (
            real * turn_cos - imaginary * turn_sin,
            real * turn_sin + imaginary * turn_cos,
        )
        middle = pltpu.roll(real[0:1], 64, 1)
        for c in range(2):
            for i in range(4):
                send2[trial, pl.ds(2 * i + c, 64, stride=8), :] = parts[c][64 * i : 64 * i + 64]
            packed = jnp.where(lane1 < 64, parts[c][0:1], pltpu.roll(parts[c][256:257], 64, 1))
            if c == 1:
                packed = jnp.where(lane1 == 0, middle, packed)
            send2[trial, c : c + 1, :] = packed

    def finish(trial):
        r_high, r_low = split(recv2[trial])
        final = product(v_last_high[...], v_last_low[...], r_high, r_low)
        power = powers.at[trial]
        power[...] = final[0:64] ** 2 + final[64:128] ** 2
        special = final[128:144] ** 2 + final[144:160] ** 2

        @pl.when(me == 0)
        def _():
            for sign in range(2):
                where = pl.ds(4 * sign, 8, stride=8)
                power[where, :] = jnp.where(
                    lane8 == 0, special[8 * sign : 8 * sign + 8], power[where, :]
                )
            for p in range(8):
                x = power[8 * p : 8 * p + 8, :]
                one = lanes_at(
                    pltpu.roll(x, 7, 0), jnp.where(sub8 == 7, lane8 + 64, 127 - lane8) & 127
                )
                two = lanes_at(
                    jnp.where(sub8 == 0, pltpu.roll(x, 4, 0), pltpu.roll(x, 3, 0)),
                    jnp.where(sub8 == 0, (128 - lane8) & 63, (191 - lane8) & 127),
                )
                head = jnp.where((sub8 == 0) & (lane8 >= 64), two, x)
                tail = jnp.where((sub8 == 7) & (lane8 >= 64), two, one)
                power[8 * p : 8 * p + 8, :] = jnp.where(sub8 < 4, head, tail)

        @pl.when(me != 0)
        def _():
            for p in range(8):
                x = power[8 * p : 8 * p + 8, :]
                power[8 * p : 8 * p + 8, :] = jnp.where(sub8 < 4, x, lanes_at(x, 127 - lane8))

        for n in range(8):
            rows_a[trial, 8 * n : 8 * n + 8, :] = power[pl.ds(n, 8, stride=8), :]

    def residue(sign):
        return me if sign == 0 else (SLOTS - me) & (SLOTS - 1)

    class_of = jnp.where(sub8 < 4, me, (SLOTS - me) & (SLOTS - 1)) + 64 * jnp.where(
        sub8 < 4, sub8, 11 - sub8
    )

    def select(trial, m, odd, shift, half):
        k1 = (INVERSE[odd] * (class_of >> shift)) & ((FIRST >> shift) - 1)
        index = ((m * k1) >> 9) + odd * (128 * half + lane8)
        total = jnp.zeros((8, 128), f32)
        for p in range(odd * half, odd * half + odd):
            total = jnp.where(
                (index >> 7) == p,
                lanes_at(powers[trial, 8 * p : 8 * p + 8, :], index & 127),
                total,
            )
        return total

    started = []

    def share(trial):
        power, by_row, term = powers.at[trial], rows_a.at[trial], terms.at[trial]
        number = [0]

        def give(source, start, m, sign, rows, to, condition):
            base = BASES[m] + (0 if m == 8 else rows * sign)
            from_ref = source.at[pl.ds(start, rows)]
            to_ref = received.at[trial, pl.ds(base, rows)]
            copy = pltpu.make_async_remote_copy(
                src_ref=from_ref, dst_ref=to_ref,
                send_sem=term_send.at[trial, number[0]], recv_sem=term_recv.at[trial],
                device_id={"fft": to}, device_id_type=mesh_id,
            )
            number[0] += 1
            away = condition & (to != me)

            @pl.when(away)
            def _():
                copy.start()

            @pl.when(condition & (to == me))
            def _():
                pltpu.make_async_copy(from_ref, to_ref, term_recv.at[trial]).start()

            started.append((copy, away))

        always, even = me >= 0, (me & 1) == 0
        for sign in range(2):
            rest = residue(sign)
            give(power, 0, 1, sign, 8, rest, always)
            for v in range(2):
                give(power, 0, 2, sign, 16, ((rest >> 1) + 32 * v) & 63, even)
            for i in range(4):
                place = i if sign == 0 else 7 - i
                at = 32 * sign + 8 * i
                give(by_row, at, 4, sign, 8, ((rest >> 2) + 16 * place) & 63, (me & 3) == 0)
                give(by_row, at, 8, sign, 8, ((rest >> 3) + 8 * place) & 63, (me & 7) == 0)
        for n, m in enumerate((3, 5, 7)):
            term[8 * n : 8 * n + 8, :] = select(trial, m, m, 0, 0)
            for sign in range(2):
                give(term, 8 * n, m, sign, 8, (INVERSE[m] * residue(sign)) & 63, always)
        for half in range(2):
            term[24 + 8 * half : 32 + 8 * half, :] = select(trial, 6, 3, 1, half)
        for sign in range(2):
            for v in range(2):
                to = (INVERSE[3] * ((residue(sign) >> 1) + 32 * v)) & 63
                give(term, 24, 6, sign, 16, to, even)

    def source_row(m, v, rows):
        place = (((m * me) >> 6) + m * v) & 7
        sign = place >> 2
        slot = jnp.where(sign == 1, 7 - place, place)
        return BASES[m] + (rows + 4) * sign + slot

    def collect(trial):
        def row_at(index):
            return received[trial, pl.ds(index, 1), :]

        total = received[trial, pl.ds(BASES[8], 8), :]
        for v in range(2):
            base = BASES[4] + 8 * v
            values = jnp.broadcast_to(row_at(base), (8, 128))
            for p in range(1, 4):
                values = jnp.where((sub8 >> 1) == p, row_at(base + p), values)
            values = lanes_at(values, 64 * (sub8 & 1) + (lane8 >> 1))
            total = total + jnp.where((lane8 & 1) == v, values, 0.0)
        for v in range(4):
            at2, at6 = source_row(2, v, 16), source_row(6, v, 16)
            low = row_at(at2) + row_at(at6)
            high = row_at(at2 + 8) + row_at(at6 + 8)
            values = jnp.where((sub8 >> 2) == 0, low, high)
            values = lanes_at(values, 32 * (sub8 & 3) + (lane8 >> 2))
            total = total + jnp.where((lane8 & 3) == v, values, 0.0)
        for v in range(8):
            values = row_at(source_row(1, v, 8))
            for m in (3, 5, 7):
                values = values + row_at(source_row(m, v, 8))
            values = lanes_at(jnp.broadcast_to(values, (8, 128)), 16 * sub8 + (lane8 >> 3))
            total = total + jnp.where((lane8 & 7) == v, values, 0.0)
        out[trial] = total * (0.125 / LENGTH)

    for trial in range(2):
        arrived(recv1.at[trial], recv1_sem.at[trial])
        transform(trial)
        exchange(send2.at[trial], recv2.at[trial], send2_sem.at[trial], recv2_sem.at[trial])
    for trial in range(2):
        arrived(recv2.at[trial], recv2_sem.at[trial])
        finish(trial)
        share(trial)
    for trial in range(2):
        arrived(received.at[trial], term_recv.at[trial])
        collect(trial)

    @pl.when(me < SLOTS - 1)
    def _():
        to_next.wait_send()

    @pl.when(me > 0)
    def _():
        to_last.wait_send()

    for trial in range(2):
        sent(send1.at[trial], send1_sem.at[trial])
        sent(send2.at[trial], send2_sem.at[trial])
    for copy, away in started:

        @pl.when(away)
        def _(copy=copy):
            copy.wait_send()


def on_device(series, filters, delays, phases):
    tables = [jnp.asarray(table) for table in make_tables()]
    whole = pl.BlockSpec(memory_space=pltpu.VMEM)
    anywhere = pl.BlockSpec(memory_space=pl.ANY)
    f32 = jnp.float32
    out = pl.pallas_call(
        kernel,
        out_shape=jax.ShapeDtypeStruct((2, 8, 128), f32),
        in_specs=[anywhere, whole, whole, whole] + [anywhere] * len(tables),
        out_specs=whole,
        scratch_shapes=[
            pltpu.VMEM((528, 128), f32),
            pltpu.VMEM((32, 256), f32),
            pltpu.VMEM((8, 256, 128), jnp.bfloat16),
            pltpu.VMEM((8, 256, 128), jnp.bfloat16),
            pltpu.VMEM((2, 512, 128), f32),
            pltpu.VMEM((2, 512, 128), f32),
            pltpu.VMEM((2, 512, 128), f32),
            pltpu.VMEM((2, 512, 128), f32),
            pltpu.VMEM((2 * FREQS, 128), f32),
            pltpu.VMEM((2, FREQS, 128), f32),
            pltpu.VMEM((2, 64, 128), f32),
            pltpu.VMEM((2, 64, 128), f32),
            pltpu.VMEM((2, 40, 128), f32),
            pltpu.VMEM((2, TERM_ROWS, 128), f32),
        ]
        + [pltpu.VMEM(table.shape, table.dtype) for table in tables]
        + [
            pltpu.SemaphoreType.DMA((len(tables),)),
            pltpu.SemaphoreType.DMA,
            pltpu.SemaphoreType.DMA((2,)),
            pltpu.SemaphoreType.DMA((2,)),
            pltpu.SemaphoreType.DMA((2,)),
            pltpu.SemaphoreType.DMA((2,)),
            pltpu.SemaphoreType.DMA((2,)),
            pltpu.SemaphoreType.DMA((2,)),
            pltpu.SemaphoreType.DMA((2, 32)),
            pltpu.SemaphoreType.DMA((2,)),
        ],
        compiler_params=pltpu.CompilerParams(
            collective_id=0, has_side_effects=True
        ),
    )(series.reshape(512, 128), delays, phases, filters.T, *tables)
    return out.reshape(2, 1, 1024)


def solution(mesh):
    return jax.shard_map(
        on_device,
        mesh=mesh,
        in_specs=(P(("dm", "fft")), P(), P(None, "fft"), P(None, "fft")),
        out_specs=P("dm", "fft", None),
        check_vma=False,
    )
```

```python
import jax
import jax.numpy as jnp
import ml_dtypes
import numpy as np
from jax import lax
from jax.experimental import pallas as pl
from jax.experimental.pallas import tpu as pltpu
from jax.sharding import PartitionSpec as P

LENGTH = 4194304
SLOTS = 64
TAPS = 16
PHASES = 32
FIRST = 512
SECOND = 128
FREQS = 272
INVERSE = {1: 1, 3: 171, 5: 205, 7: 439}
BASES = {1: 0, 3: 16, 5: 32, 7: 48, 2: 64, 6: 96, 4: 128, 8: 144}
TERM_ROWS = 152


def split_table(table):
    table = np.asarray(table, np.float32)
    high = table.astype(ml_dtypes.bfloat16)
    low = (table - high.astype(np.float32)).astype(ml_dtypes.bfloat16)
    return high, low


def make_tables():
    turn = 2.0 * np.pi
    angle = turn / FIRST * (np.arange(FREQS)[:, None] * np.arange(FIRST)[None, :] % FIRST)
    first = np.concatenate([np.cos(angle), -np.sin(angle)], axis=0)
    h, rr, c_hi = np.meshgrid(np.arange(2), np.arange(2), np.arange(32), indexing="ij")
    second_index = (64 * rr + 2 * c_hi + h).reshape(-1)
    angle = turn / 65536 * (np.arange(FREQS)[:, None] * second_index[None, :] % 65536)
    mid = np.stack([np.cos(angle), -np.sin(angle)]).astype(np.float32)
    angle = turn / SECOND * (second_index[:, None] * np.arange(SECOND)[None, :] % SECOND)
    cos_part, sin_part = np.cos(angle), np.sin(angle)
    second = np.block([[cos_part, -sin_part], [sin_part, cos_part]])
    angle = turn / LENGTH * (np.arange(FREQS)[:, None] * np.arange(128)[None, :])
    col = np.stack([np.cos(angle), -np.sin(angle)]).astype(np.float32)
    angle = turn / 8192 * (np.arange(SLOTS)[:, None] * np.arange(SECOND)[None, :] % 8192)
    row = np.stack([np.cos(angle), -np.sin(angle)]).astype(np.float32)
    last = np.zeros((2, 8, 2, 4, SLOTS, 4, 2))
    special = np.zeros((2, 2, 8, SLOTS, 4, 2))
    q = np.arange(SLOTS)
    for sign in range(2):
        for p in range(8):
            actual = p if sign == 0 else -1 - p
            theta = turn / 64 * (q * actual % 64)
            for i in range(4):
                last[0, p, sign, i, :, i, 0] = np.cos(theta)
                last[0, p, sign, i, :, i, 1] = np.sin(theta)
                last[1, p, sign, i, :, i, 0] = -np.sin(theta)
                last[1, p, sign, i, :, i, 1] = np.cos(theta)
            theta = turn / 128 * (q * (2 * p + sign) % 128)
            special[0, sign, p, :, 0, sign] = np.cos(theta)
            special[1, sign, p, :, 0, sign] = -np.sin(theta)
    last = np.concatenate([last.reshape(128, 512), special.reshape(32, 512)], axis=0)
    return (*split_table(first), *split_table(second), *split_table(last), mid, col, row)


def split(x):
    high = x.astype(jnp.bfloat16)
    return high, (x - high.astype(jnp.float32)).astype(jnp.bfloat16)


def dot(a, b):
    return jnp.dot(a, b, preferred_element_type=jnp.float32)


def product(a_high, a_low, b_high, b_low):
    wide = dot(a_high, jnp.concatenate([b_high, b_low], 1))
    return wide[:, 0:128] + wide[:, 128:256] + dot(a_low, b_high)


def lanes_at(x, index):
    return jnp.take_along_axis(x, index, axis=1, mode="promise_in_bounds")


def iota(shape, axis):
    return lax.broadcasted_iota(jnp.int32, shape, axis)


def column_of(values, own, second_trial):
    chosen = jnp.where(second_trial, values[1:2, :], values[0:1, :])
    return jnp.sum(jnp.where(own, chosen, 0.0), axis=1, keepdims=True)


def kernel(
    series, delays, phases, filters,
    first_high, first_low, second_high, second_low, last_high, last_low, mid, col, row,
    out,
    v_delays, v_phases, v_filters, ext, halos, fixes, fixed, responses, windows_high, windows_low, send1, recv1, send2, recv2, spectrum, turn,
    powers, rows_a, terms, received,
    v_first_high, v_first_low, v_second_high, v_second_low, v_last_high, v_last_low,
    v_mid, v_col, v_row,
    small_sem, table_sem, series_sem, halo_send, halo_recv, fix_sem,
    send1_sem, recv1_sem, send2_sem, recv2_sem, term_send, term_recv,
):
    me = lax.axis_index("fft")
    f32 = jnp.float32
    mesh_id = pl.DeviceIdType.MESH

    barrier = pltpu.get_barrier_semaphore()

    def partners(act):
        def partner(dz, dy, dc):
            y, z = ((me >> 4) + dy) & 3, ((me >> 1) + dz) & 7
            act((y << 4) + (z << 1) + ((me & 1) ^ dc))

        def ring(step, carry):
            side = jnp.where((step & 1) == 1, (step + 1) >> 1, -(step >> 1))
            for dy in (2, 1, 3, 0):
                for dc in range(2):
                    partner(4 + side, dy, dc)
            return carry

        lax.fori_loop(0, 7, ring, 0)
        for dy in (2, 1, 3, 0):
            for dc in range(2):
                if dy or dc:
                    partner(0, dy, dc)

    def greet(to):
        pl.semaphore_signal(barrier, inc=1, device_id={"fft": to}, device_id_type=mesh_id)

    small = [
        pltpu.make_async_copy(source, target, small_sem.at[n])
        for n, (source, target) in enumerate(
            ((delays, v_delays), (phases, v_phases), (filters, v_filters))
        )
    ]
    for copy in small:
        copy.start()
    partners(greet)
    own_series = pltpu.make_async_copy(series, ext.at[pl.ds(8, 512)], series_sem)
    own_series.start()
    tables = [
        pltpu.make_async_copy(source, target, table_sem.at[n])
        for n, (source, target) in enumerate(
            (
                (first_high, v_first_high), (first_low, v_first_low),
                (second_high, v_second_high), (second_low, v_second_low),
                (last_high, v_last_high), (last_low, v_last_low),
                (mid, v_mid), (col, v_col), (row, v_row),
            )
        )
    ]
    for copy in tables:
        copy.start()

    for copy in small:
        copy.wait()
    line = iota((32, 16), 0)
    own = iota((32, 16), 1) == 2 * (line >> 2) + (line & 1)
    second_trial = ((line >> 1) & 1) == 1
    delay = column_of(v_delays[...].astype(f32), own, second_trial)
    phase = column_of(v_phases[...].astype(f32), own, second_trial)
    branch = (iota((32, PHASES), 1).astype(f32) == phase).astype(f32)
    taps = lax.dot_general(
        branch, v_filters[...], (((1,), (1,)), ((), ())),
        precision=lax.Precision.HIGHEST, preferred_element_type=f32,
    )
    position = iota((32, 256), 1).astype(f32) - (delay + 56.0)
    response = jnp.zeros((32, 256), f32)
    for tap in range(TAPS):
        response = jnp.where(position == float(tap), taps[:, tap : tap + 1], response)
    responses[...] = response

    own_series.wait()
    ext[0:8, :] = jnp.zeros((8, 128), f32)
    ext[520:528, :] = jnp.zeros((8, 128), f32)

    lane64 = iota((64, 128), 1)

    def resample(trial, rg):
        if trial == 0:
            before = ext[pl.ds(64 * rg + 7, 64), :]
            here = ext[pl.ds(64 * rg + 8, 64), :]
            after = ext[pl.ds(64 * rg + 9, 64), :]
            left = pltpu.roll(jnp.where(lane64 < 64, here, before), 64, 1)
            right = pltpu.roll(jnp.where(lane64 < 64, after, here), 64, 1)
            window = jnp.concatenate(
                [jnp.concatenate([left, here], 0).T, jnp.concatenate([right, after], 0).T], 0
            )
            w_high, w_low = split(window)
            windows_high[rg], windows_low[rg] = w_high, w_low
        else:
            w_high, w_low = windows_high[rg], windows_low[rg]
        bands = []
        for rr in range(2):
            line = responses[pl.ds(4 * rg + 2 * trial + rr, 1), :]
            bands.append(
                pltpu.roll(jnp.broadcast_to(line, (64, 256)), 0, 1, stride=1, stride_axis=0)
            )
        b_high, b_low = split(jnp.concatenate(bands, 0))
        both = product(b_high, b_low, w_high, w_low)
        return jnp.where((lane64 & 32) == 0, both[0:64], both[64:128])

    def exchange(source, target, send_sem, recv_sem, rows=8):
        mine = pl.ds(pl.multiple_of(8 * me, 8), rows)

        def send(to):
            pltpu.make_async_remote_copy(
                src_ref=source.at[pl.ds(pl.multiple_of(8 * to, 8), rows)],
                dst_ref=target.at[mine],
                send_sem=send_sem, recv_sem=recv_sem,
                device_id={"fft": to}, device_id_type=mesh_id,
            ).start()

        partners(send)
        pltpu.make_async_copy(source.at[mine], target.at[mine], recv_sem).start()

    def arrived(target, sem):
        pltpu.make_async_copy(target, target, sem).wait()

    def sent(source, sem, rows=8):
        part = source.at[pl.ds(0, rows * (SLOTS - 1))]
        pltpu.make_async_copy(part, part, sem).wait()

    def inner(trial):
        def body(rg, carry):
            send1[trial, pl.ds(rg, 64, stride=8), :] = resample(trial, rg)
            return carry

        return body

    lax.fori_loop(0, 8, inner(0), 0)
    lax.fori_loop(1, 7, inner(1), 0)
    pl.semaphore_wait(barrier, SLOTS - 1)
    to_next = pltpu.make_async_remote_copy(
        src_ref=series.at[pl.ds(504, 8)], dst_ref=halos.at[0],
        send_sem=halo_send.at[0], recv_sem=halo_recv.at[0],
        device_id={"fft": (me + 1) & (SLOTS - 1)}, device_id_type=mesh_id,
    )
    to_last = pltpu.make_async_remote_copy(
        src_ref=series.at[pl.ds(0, 8)], dst_ref=halos.at[1],
        send_sem=halo_send.at[1], recv_sem=halo_recv.at[1],
        device_id={"fft": (me + SLOTS - 1) & (SLOTS - 1)}, device_id_type=mesh_id,
    )

    @pl.when(me < SLOTS - 1)
    def _():
        to_next.start()

    @pl.when(me > 0)
    def _():
        to_last.start()

    exchange(send1.at[0], recv1.at[0], send1_sem.at[0], recv1_sem.at[0])

    @pl.when(me > 0)
    def _():
        to_next.wait_recv()
        ext[0:8, :] = halos[0]

    @pl.when(me < SLOTS - 1)
    def _():
        to_last.wait_recv()
        ext[520:528, :] = halos[1]

    fixes[pl.ds(0, 64, stride=8), :] = jnp.where(lane64 == 0, resample(0, 0), resample(0, 7))
    exchange(fixes, fixed, fix_sem.at[0], fix_sem.at[1], 1)
    for rg in (0, 7):
        send1[1, pl.ds(rg, 64, stride=8), :] = resample(1, rg)
    exchange(send1.at[1], recv1.at[1], send1_sem.at[1], recv1_sem.at[1])

    for copy in tables:
        copy.wait()
    me_lane = iota((FREQS, 128), 1) == me
    col_cos = jnp.sum(jnp.where(me_lane, v_col[0], 0.0), axis=1, keepdims=True)
    col_sin = jnp.sum(jnp.where(me_lane, v_col[1], 0.0), axis=1, keepdims=True)
    row_cos = v_row[0, pl.ds(me, 1), :]
    row_sin = v_row[1, pl.ds(me, 1), :]
    turn[0] = col_cos * row_cos - col_sin * row_sin
    turn[1] = col_cos * row_sin + col_sin * row_cos
    lane1 = iota((1, 128), 1)
    lane8, sub8 = iota((8, 128), 1), iota((8, 128), 0)

    def transform(trial):
        d_high, d_low = split(recv1[trial])
        spectrum[...] = product(v_first_high[...], v_first_low[...], d_high, d_low)
        real, imaginary = spectrum[0:FREQS, :], spectrum[FREQS : 2 * FREQS, :]
        mid_cos, mid_sin = v_mid[0], v_mid[1]
        turned = jnp.concatenate(
            [real * mid_cos - imaginary * mid_sin, real * mid_sin + imaginary * mid_cos], 1
        )
        t_high, t_low = split(turned)
        s_high = v_second_high[...]
        result = dot(t_high, s_high) + dot(t_low, s_high) + dot(t_high, v_second_low[...])
        real, imaginary = result[:, 0:128], result[:, 128:256]
        turn_cos, turn_sin = turn[0], turn[1]
        parts = (
            real * turn_cos - imaginary * turn_sin,
            real * turn_sin + imaginary * turn_cos,
        )
        middle = pltpu.roll(real[0:1], 64, 1)
        for c in range(2):
            for i in range(4):
                send2[trial, pl.ds(2 * i + c, 64, stride=8), :] = parts[c][64 * i : 64 * i + 64]
            packed = jnp.where(lane1 < 64, parts[c][0:1], pltpu.roll(parts[c][256:257], 64, 1))
            if c == 1:
                packed = jnp.where(lane1 == 0, middle, packed)
            send2[trial, c : c + 1, :] = packed

    def finish(trial):
        r_high, r_low = split(recv2[trial])
        final = product(v_last_high[...], v_last_low[...], r_high, r_low)
        power = powers.at[trial]
        power[...] = final[0:64] ** 2 + final[64:128] ** 2
        special = final[128:144] ** 2 + final[144:160] ** 2

        @pl.when(me == 0)
        def _():
            for sign in range(2):
                where = pl.ds(4 * sign, 8, stride=8)
                power[where, :] = jnp.where(
                    lane8 == 0, special[8 * sign : 8 * sign + 8], power[where, :]
                )
            for p in range(8):
                x = power[8 * p : 8 * p + 8, :]
                one = lanes_at(
                    pltpu.roll(x, 7, 0), jnp.where(sub8 == 7, lane8 + 64, 127 - lane8) & 127
                )
                two = lanes_at(
                    jnp.where(sub8 == 0, pltpu.roll(x, 4, 0), pltpu.roll(x, 3, 0)),
                    jnp.where(sub8 == 0, (128 - lane8) & 63, (191 - lane8) & 127),
                )
                head = jnp.where((sub8 == 0) & (lane8 >= 64), two, x)
                tail = jnp.where((sub8 == 7) & (lane8 >= 64), two, one)
                power[8 * p : 8 * p + 8, :] = jnp.where(sub8 < 4, head, tail)

        @pl.when(me != 0)
        def _():
            for p in range(8):
                x = power[8 * p : 8 * p + 8, :]
                power[8 * p : 8 * p + 8, :] = jnp.where(sub8 < 4, x, lanes_at(x, 127 - lane8))

        for n in range(8):
            rows_a[trial, 8 * n : 8 * n + 8, :] = power[pl.ds(n, 8, stride=8), :]

    def residue(sign):
        return me if sign == 0 else (SLOTS - me) & (SLOTS - 1)

    class_of = jnp.where(sub8 < 4, me, (SLOTS - me) & (SLOTS - 1)) + 64 * jnp.where(
        sub8 < 4, sub8, 11 - sub8
    )

    def select(trial, m, odd, shift, half):
        k1 = (INVERSE[odd] * (class_of >> shift)) & ((FIRST >> shift) - 1)
        index = ((m * k1) >> 9) + odd * (128 * half + lane8)
        total = jnp.zeros((8, 128), f32)
        for p in range(odd * half, odd * half + odd):
            total = jnp.where(
                (index >> 7) == p,
                lanes_at(powers[trial, 8 * p : 8 * p + 8, :], index & 127),
                total,
            )
        return total

    started = []

    def share(trial):
        power, by_row, term = powers.at[trial], rows_a.at[trial], terms.at[trial]
        number = [0]

        def give(source, start, m, sign, rows, to, condition):
            base = BASES[m] + (0 if m == 8 else rows * sign)
            from_ref = source.at[pl.ds(start, rows)]
            to_ref = received.at[trial, pl.ds(base, rows)]
            copy = pltpu.make_async_remote_copy(
                src_ref=from_ref, dst_ref=to_ref,
                send_sem=term_send.at[trial, number[0]], recv_sem=term_recv.at[trial],
                device_id={"fft": to}, device_id_type=mesh_id,
            )
            number[0] += 1
            away = condition & (to != me)

            @pl.when(away)
            def _():
                copy.start()

            @pl.when(condition & (to == me))
            def _():
                pltpu.make_async_copy(from_ref, to_ref, term_recv.at[trial]).start()

            started.append((copy, away))

        always, even = me >= 0, (me & 1) == 0
        for sign in range(2):
            rest = residue(sign)
            give(power, 0, 1, sign, 8, rest, always)
            for v in range(2):
                give(power, 0, 2, sign, 16, ((rest >> 1) + 32 * v) & 63, even)
            for i in range(4):
                place = i if sign == 0 else 7 - i
                at = 32 * sign + 8 * i
                give(by_row, at, 4, sign, 8, ((rest >> 2) + 16 * place) & 63, (me & 3) == 0)
                give(by_row, at, 8, sign, 8, ((rest >> 3) + 8 * place) & 63, (me & 7) == 0)
        for n, m in enumerate((3, 5, 7)):
            term[8 * n : 8 * n + 8, :] = select(trial, m, m, 0, 0)
            for sign in range(2):
                give(term, 8 * n, m, sign, 8, (INVERSE[m] * residue(sign)) & 63, always)
        for half in range(2):
            term[24 + 8 * half : 32 + 8 * half, :] = select(trial, 6, 3, 1, half)
        for sign in range(2):
            for v in range(2):
                to = (INVERSE[3] * ((residue(sign) >> 1) + 32 * v)) & 63
                give(term, 24, 6, sign, 16, to, even)

    def source_row(m, v, rows):
        place = (((m * me) >> 6) + m * v) & 7
        sign = place >> 2
        slot = jnp.where(sign == 1, 7 - place, place)
        return BASES[m] + (rows + 4) * sign + slot

    def collect(trial):
        def row_at(index):
            return received[trial, pl.ds(index, 1), :]

        total = received[trial, pl.ds(BASES[8], 8), :]
        for v in range(2):
            base = BASES[4] + 8 * v
            values = jnp.broadcast_to(row_at(base), (8, 128))
            for p in range(1, 4):
                values = jnp.where((sub8 >> 1) == p, row_at(base + p), values)
            values = lanes_at(values, 64 * (sub8 & 1) + (lane8 >> 1))
            total = total + jnp.where((lane8 & 1) == v, values, 0.0)
        for v in range(4):
            at2, at6 = source_row(2, v, 16), source_row(6, v, 16)
            low = row_at(at2) + row_at(at6)
            high = row_at(at2 + 8) + row_at(at6 + 8)
            values = jnp.where((sub8 >> 2) == 0, low, high)
            values = lanes_at(values, 32 * (sub8 & 3) + (lane8 >> 2))
            total = total + jnp.where((lane8 & 3) == v, values, 0.0)
        for v in range(8):
            values = row_at(source_row(1, v, 8))
            for m in (3, 5, 7):
                values = values + row_at(source_row(m, v, 8))
            values = lanes_at(jnp.broadcast_to(values, (8, 128)), 16 * sub8 + (lane8 >> 3))
            total = total + jnp.where((lane8 & 7) == v, values, 0.0)
        out[trial] = total * (0.125 / LENGTH)

    for trial in range(2):
        arrived(recv1.at[trial], recv1_sem.at[trial])
        if trial == 0:
            arrived(fixed.at[pl.ds(0, SLOTS)], fix_sem.at[1])
            right = fixed[pl.ds(0, 64, stride=8), :]
            for rg, at in ((0, 0), (7, 127)):
                where = pl.ds(rg, 64, stride=8)
                recv1[0, where, :] = jnp.where(lane64 == at, right, recv1[0, where, :])
        transform(trial)
        exchange(send2.at[trial], recv2.at[trial], send2_sem.at[trial], recv2_sem.at[trial])
    for trial in range(2):
        arrived(recv2.at[trial], recv2_sem.at[trial])
        finish(trial)
        share(trial)
    arrived(received.at[0], term_recv.at[0])
    collect(0)

    @pl.when(me < SLOTS - 1)
    def _():
        to_next.wait_send()

    @pl.when(me > 0)
    def _():
        to_last.wait_send()

    sent(fixes, fix_sem.at[0], 1)
    for trial in range(2):
        sent(send1.at[trial], send1_sem.at[trial])
        sent(send2.at[trial], send2_sem.at[trial])
    for copy, away in started:

        @pl.when(away)
        def _(copy=copy):
            copy.wait_send()

    arrived(received.at[1], term_recv.at[1])
    collect(1)


def on_device(series, filters, delays, phases):
    tables = [jnp.asarray(table) for table in make_tables()]
    whole = pl.BlockSpec(memory_space=pltpu.VMEM)
    anywhere = pl.BlockSpec(memory_space=pl.ANY)
    f32 = jnp.float32
    out = pl.pallas_call(
        kernel,
        out_shape=jax.ShapeDtypeStruct((2, 8, 128), f32),
        in_specs=[anywhere] * (4 + len(tables)),
        out_specs=whole,
        scratch_shapes=[
            pltpu.VMEM((2, 16), jnp.int32),
            pltpu.VMEM((2, 16), jnp.int32),
            pltpu.VMEM((TAPS, PHASES), f32),
            pltpu.VMEM((528, 128), f32),
            pltpu.VMEM((2, 8, 128), f32),
            pltpu.VMEM((512, 128), f32),
            pltpu.VMEM((512, 128), f32),
            pltpu.VMEM((32, 256), f32),
            pltpu.VMEM((8, 256, 128), jnp.bfloat16),
            pltpu.VMEM((8, 256, 128), jnp.bfloat16),
            pltpu.VMEM((2, 512, 128), f32),
            pltpu.VMEM((2, 512, 128), f32),
            pltpu.VMEM((2, 512, 128), f32),
            pltpu.VMEM((2, 512, 128), f32),
            pltpu.VMEM((2 * FREQS, 128), f32),
            pltpu.VMEM((2, FREQS, 128), f32),
            pltpu.VMEM((2, 64, 128), f32),
            pltpu.VMEM((2, 64, 128), f32),
            pltpu.VMEM((2, 40, 128), f32),
            pltpu.VMEM((2, TERM_ROWS, 128), f32),
        ]
        + [pltpu.VMEM(table.shape, table.dtype) for table in tables]
        + [
            pltpu.SemaphoreType.DMA((3,)),
            pltpu.SemaphoreType.DMA((len(tables),)),
            pltpu.SemaphoreType.DMA,
            pltpu.SemaphoreType.DMA((2,)),
            pltpu.SemaphoreType.DMA((2,)),
            pltpu.SemaphoreType.DMA((2,)),
            pltpu.SemaphoreType.DMA((2,)),
            pltpu.SemaphoreType.DMA((2,)),
            pltpu.SemaphoreType.DMA((2,)),
            pltpu.SemaphoreType.DMA((2,)),
            pltpu.SemaphoreType.DMA((2, 32)),
            pltpu.SemaphoreType.DMA((2,)),
        ],
        compiler_params=pltpu.CompilerParams(
            collective_id=0, has_side_effects=True
        ),
    )(series.reshape(512, 128), delays, phases, filters.T, *tables)
    return out.reshape(2, 1, 1024)


def solution(mesh):
    return jax.shard_map(
        on_device,
        mesh=mesh,
        in_specs=(P(("dm", "fft")), P(), P(None, "fft"), P(None, "fft")),
        out_specs=P("dm", "fft", None),
        check_vma=False,
    )
```

```python
import jax
import jax.numpy as jnp
import ml_dtypes
import numpy as np
from jax import lax
from jax.experimental import pallas as pl
from jax.experimental.pallas import tpu as pltpu
from jax.sharding import PartitionSpec as P

LENGTH = 4194304
SLOTS = 64
TAPS = 16
PHASES = 32
FIRST = 512
SECOND = 128
FREQS = 272
INVERSE = {1: 1, 3: 171, 5: 205, 7: 439}
BASES = {1: 0, 3: 16, 5: 32, 7: 48, 2: 64, 6: 96, 4: 128, 8: 144}
TERM_ROWS = 152
PAIRS = (
    6, 16, 3, 24, 18, 22, 2, 15, 5, 4, 21, 12, 28, 17, 31, 8,
    7, 9, 20, 19, 25, 11, 13, 26, 0, 30, 14, 10, 23, 29, 27, 1,
)


def split_table(table):
    table = np.asarray(table, np.float32)
    high = table.astype(ml_dtypes.bfloat16)
    low = (table - high.astype(np.float32)).astype(ml_dtypes.bfloat16)
    return high, low


def make_tables():
    turn = 2.0 * np.pi
    angle = turn / FIRST * (np.arange(FREQS)[:, None] * np.arange(FIRST)[None, :] % FIRST)
    first = np.concatenate([np.cos(angle), -np.sin(angle)], axis=0)
    h, rr, c_hi = np.meshgrid(np.arange(2), np.arange(2), np.arange(32), indexing="ij")
    second_index = (64 * rr + 2 * c_hi + h).reshape(-1)
    angle = turn / 65536 * (np.arange(FREQS)[:, None] * second_index[None, :] % 65536)
    mid = np.stack([np.cos(angle), -np.sin(angle)]).astype(np.float32)
    angle = turn / SECOND * (second_index[:, None] * np.arange(SECOND)[None, :] % SECOND)
    cos_part, sin_part = np.cos(angle), np.sin(angle)
    second = np.block([[cos_part, -sin_part], [sin_part, cos_part]])
    angle = turn / LENGTH * (np.arange(FREQS)[:, None] * np.arange(128)[None, :])
    col = np.stack([np.cos(angle), -np.sin(angle)]).astype(np.float32)
    angle = turn / 8192 * (np.arange(SLOTS)[:, None] * np.arange(SECOND)[None, :] % 8192)
    row = np.stack([np.cos(angle), -np.sin(angle)]).astype(np.float32)
    last = np.zeros((2, 8, 2, 4, SLOTS, 4, 2))
    special = np.zeros((2, 2, 8, SLOTS, 4, 2))
    q = np.arange(SLOTS)
    for sign in range(2):
        for p in range(8):
            actual = p if sign == 0 else -1 - p
            theta = turn / 64 * (q * actual % 64)
            for i in range(4):
                last[0, p, sign, i, :, i, 0] = np.cos(theta)
                last[0, p, sign, i, :, i, 1] = np.sin(theta)
                last[1, p, sign, i, :, i, 0] = -np.sin(theta)
                last[1, p, sign, i, :, i, 1] = np.cos(theta)
            theta = turn / 128 * (q * (2 * p + sign) % 128)
            special[0, sign, p, :, 0, sign] = np.cos(theta)
            special[1, sign, p, :, 0, sign] = -np.sin(theta)
    last = np.concatenate([last.reshape(128, 512), special.reshape(32, 512)], axis=0)
    return (*split_table(first), *split_table(second), *split_table(last), mid, col, row)


def split(x):
    high = x.astype(jnp.bfloat16)
    return high, (x - high.astype(jnp.float32)).astype(jnp.bfloat16)


def dot(a, b):
    return jnp.dot(a, b, preferred_element_type=jnp.float32)


def product(a_high, a_low, b_high, b_low):
    wide = dot(a_high, jnp.concatenate([b_high, b_low], 1))
    return wide[:, 0:128] + wide[:, 128:256] + dot(a_low, b_high)


def lanes_at(x, index):
    return jnp.take_along_axis(x, index, axis=1, mode="promise_in_bounds")


def iota(shape, axis):
    return lax.broadcasted_iota(jnp.int32, shape, axis)


def class_at(device):
    words = [sum(PAIRS[4 * n + b] << (8 * b) for b in range(4)) for n in range(8)]
    chip = device >> 1
    word = jnp.int32(words[0])
    for n in range(1, 8):
        word = jnp.where((chip >> 2) == n, jnp.int32(words[n]), word)
    pair = (word >> ((chip & 3) << 3)) & 31
    other = jnp.where(pair == 0, SLOTS // 2, SLOTS - pair)
    return jnp.where((device & 1) == 0, pair, other)


def column_of(values, own, second_trial):
    chosen = jnp.where(second_trial, values[1:2, :], values[0:1, :])
    return jnp.sum(jnp.where(own, chosen, 0.0), axis=1, keepdims=True)


def kernel(
    series, delays, phases, filters,
    first_high, first_low, second_high, second_low, last_high, last_low, mid, col, row,
    out,
    v_delays, v_phases, v_filters, ext, halos, fixes, fixed, responses, windows_high, windows_low, send1, recv1, send2, recv2, spectrum, turn,
    powers, rows_a, terms, received,
    v_first_high, v_first_low, v_second_high, v_second_low, v_last_high, v_last_low,
    v_mid, v_col, v_row,
    small_sem, table_sem, series_sem, halo_send, halo_recv, fix_sem,
    send1_sem, recv1_sem, send2_sem, recv2_sem, term_send, term_recv,
):
    me = lax.axis_index("fft")
    cls = class_at(me)
    f32 = jnp.float32
    mesh_id = pl.DeviceIdType.MESH

    barrier = pltpu.get_barrier_semaphore()

    def partners(act):
        def partner(dz, dy, dc):
            y, z = ((me >> 4) + dy) & 3, ((me >> 1) + dz) & 7
            act((y << 4) + (z << 1) + ((me & 1) ^ dc))

        for dy in (2, 1, 3, 0):
            for dc in range(2):
                for dz in (4, 3, 5, 2, 6, 1, 7, 0):
                    if dz or dy or dc:
                        partner(dz, dy, dc)

    def greet(to):
        pl.semaphore_signal(barrier, inc=1, device_id={"fft": to}, device_id_type=mesh_id)

    small = [
        pltpu.make_async_copy(source, target, small_sem.at[n])
        for n, (source, target) in enumerate(
            ((delays, v_delays), (phases, v_phases), (filters, v_filters))
        )
    ]
    for copy in small:
        copy.start()
    partners(greet)
    own_series = pltpu.make_async_copy(series, ext.at[pl.ds(8, 512)], series_sem)
    own_series.start()
    tables = [
        pltpu.make_async_copy(source, target, table_sem.at[n])
        for n, (source, target) in enumerate(
            (
                (first_high, v_first_high), (first_low, v_first_low),
                (second_high, v_second_high), (second_low, v_second_low),
                (last_high, v_last_high), (last_low, v_last_low),
                (mid, v_mid), (col, v_col), (row, v_row),
            )
        )
    ]
    for copy in tables:
        copy.start()

    for copy in small:
        copy.wait()
    line = iota((32, 16), 0)
    own = iota((32, 16), 1) == 2 * (line >> 2) + (line & 1)
    second_trial = ((line >> 1) & 1) == 1
    delay = column_of(v_delays[...].astype(f32), own, second_trial)
    phase = column_of(v_phases[...].astype(f32), own, second_trial)
    branch = (iota((32, PHASES), 1).astype(f32) == phase).astype(f32)
    taps = lax.dot_general(
        branch, v_filters[...], (((1,), (1,)), ((), ())),
        precision=lax.Precision.HIGHEST, preferred_element_type=f32,
    )
    position = iota((32, 256), 1).astype(f32) - (delay + 56.0)
    response = jnp.zeros((32, 256), f32)
    for tap in range(TAPS):
        response = jnp.where(position == float(tap), taps[:, tap : tap + 1], response)
    responses[...] = response

    own_series.wait()
    ext[0:8, :] = jnp.zeros((8, 128), f32)
    ext[520:528, :] = jnp.zeros((8, 128), f32)

    lane64 = iota((64, 128), 1)

    def resample(trial, rg):
        if trial == 0:
            before = ext[pl.ds(64 * rg + 7, 64), :]
            here = ext[pl.ds(64 * rg + 8, 64), :]
            after = ext[pl.ds(64 * rg + 9, 64), :]
            left = pltpu.roll(jnp.where(lane64 < 64, here, before), 64, 1)
            right = pltpu.roll(jnp.where(lane64 < 64, after, here), 64, 1)
            window = jnp.concatenate(
                [jnp.concatenate([left, here], 0).T, jnp.concatenate([right, after], 0).T], 0
            )
            w_high, w_low = split(window)
            windows_high[rg], windows_low[rg] = w_high, w_low
        else:
            w_high, w_low = windows_high[rg], windows_low[rg]
        bands = []
        for rr in range(2):
            line = responses[pl.ds(4 * rg + 2 * trial + rr, 1), :]
            bands.append(
                pltpu.roll(jnp.broadcast_to(line, (64, 256)), 0, 1, stride=1, stride_axis=0)
            )
        b_high, b_low = split(jnp.concatenate(bands, 0))
        both = product(b_high, b_low, w_high, w_low)
        return jnp.where((lane64 & 32) == 0, both[0:64], both[64:128])

    def exchange(source, target, send_sem, recv_sem, rows=8, block_of=lambda device: device):
        mine = pl.ds(pl.multiple_of(8 * me, 8), rows)

        def block(device):
            return source.at[pl.ds(pl.multiple_of(8 * block_of(device), 8), rows)]

        def send(to):
            pltpu.make_async_remote_copy(
                src_ref=block(to), dst_ref=target.at[mine],
                send_sem=send_sem, recv_sem=recv_sem,
                device_id={"fft": to}, device_id_type=mesh_id,
            ).start()

        partners(send)
        pltpu.make_async_copy(block(me), target.at[mine], recv_sem).start()

    def arrived(target, sem):
        pltpu.make_async_copy(target, target, sem).wait()

    def sent(source, sem, rows=8):
        part = source.at[pl.ds(0, rows * (SLOTS - 1))]
        pltpu.make_async_copy(part, part, sem).wait()

    def inner(trial):
        def body(rg, carry):
            send1[trial, pl.ds(rg, 64, stride=8), :] = resample(trial, rg)
            return carry

        return body

    lax.fori_loop(0, 8, inner(0), 0)
    lax.fori_loop(1, 7, inner(1), 0)
    pl.semaphore_wait(barrier, SLOTS - 1)
    to_next = pltpu.make_async_remote_copy(
        src_ref=series.at[pl.ds(504, 8)], dst_ref=halos.at[0],
        send_sem=halo_send.at[0], recv_sem=halo_recv.at[0],
        device_id={"fft": (me + 1) & (SLOTS - 1)}, device_id_type=mesh_id,
    )
    to_last = pltpu.make_async_remote_copy(
        src_ref=series.at[pl.ds(0, 8)], dst_ref=halos.at[1],
        send_sem=halo_send.at[1], recv_sem=halo_recv.at[1],
        device_id={"fft": (me + SLOTS - 1) & (SLOTS - 1)}, device_id_type=mesh_id,
    )

    @pl.when(me < SLOTS - 1)
    def _():
        to_next.start()

    @pl.when(me > 0)
    def _():
        to_last.start()

    exchange(send1.at[0], recv1.at[0], send1_sem.at[0], recv1_sem.at[0])

    @pl.when(me > 0)
    def _():
        to_next.wait_recv()
        ext[0:8, :] = halos[0]

    @pl.when(me < SLOTS - 1)
    def _():
        to_last.wait_recv()
        ext[520:528, :] = halos[1]

    fixes[pl.ds(0, 64, stride=8), :] = jnp.where(lane64 == 0, resample(0, 0), resample(0, 7))
    exchange(fixes, fixed, fix_sem.at[0], fix_sem.at[1], 1)
    for rg in (0, 7):
        send1[1, pl.ds(rg, 64, stride=8), :] = resample(1, rg)
    exchange(send1.at[1], recv1.at[1], send1_sem.at[1], recv1_sem.at[1])

    for copy in tables:
        copy.wait()
    me_lane = iota((FREQS, 128), 1) == me
    col_cos = jnp.sum(jnp.where(me_lane, v_col[0], 0.0), axis=1, keepdims=True)
    col_sin = jnp.sum(jnp.where(me_lane, v_col[1], 0.0), axis=1, keepdims=True)
    row_cos = v_row[0, pl.ds(me, 1), :]
    row_sin = v_row[1, pl.ds(me, 1), :]
    turn[0] = col_cos * row_cos - col_sin * row_sin
    turn[1] = col_cos * row_sin + col_sin * row_cos
    lane1 = iota((1, 128), 1)
    lane8, sub8 = iota((8, 128), 1), iota((8, 128), 0)

    def transform(trial):
        d_high, d_low = split(recv1[trial])
        spectrum[...] = product(v_first_high[...], v_first_low[...], d_high, d_low)
        real, imaginary = spectrum[0:FREQS, :], spectrum[FREQS : 2 * FREQS, :]
        mid_cos, mid_sin = v_mid[0], v_mid[1]
        turned = jnp.concatenate(
            [real * mid_cos - imaginary * mid_sin, real * mid_sin + imaginary * mid_cos], 1
        )
        t_high, t_low = split(turned)
        s_high = v_second_high[...]
        result = dot(t_high, s_high) + dot(t_low, s_high) + dot(t_high, v_second_low[...])
        real, imaginary = result[:, 0:128], result[:, 128:256]
        turn_cos, turn_sin = turn[0], turn[1]
        parts = (
            real * turn_cos - imaginary * turn_sin,
            real * turn_sin + imaginary * turn_cos,
        )
        middle = pltpu.roll(real[0:1], 64, 1)
        for c in range(2):
            for i in range(4):
                send2[trial, pl.ds(2 * i + c, 64, stride=8), :] = parts[c][64 * i : 64 * i + 64]
            packed = jnp.where(lane1 < 64, parts[c][0:1], pltpu.roll(parts[c][256:257], 64, 1))
            if c == 1:
                packed = jnp.where(lane1 == 0, middle, packed)
            send2[trial, c : c + 1, :] = packed

    def finish(trial):
        r_high, r_low = split(recv2[trial])
        final = product(v_last_high[...], v_last_low[...], r_high, r_low)
        power = powers.at[trial]
        power[...] = final[0:64] ** 2 + final[64:128] ** 2
        special = final[128:144] ** 2 + final[144:160] ** 2

        @pl.when(cls == 0)
        def _():
            for sign in range(2):
                where = pl.ds(4 * sign, 8, stride=8)
                power[where, :] = jnp.where(
                    lane8 == 0, special[8 * sign : 8 * sign + 8], power[where, :]
                )
            for p in range(8):
                x = power[8 * p : 8 * p + 8, :]
                one = lanes_at(
                    pltpu.roll(x, 7, 0), jnp.where(sub8 == 7, lane8 + 64, 127 - lane8) & 127
                )
                two = lanes_at(
                    jnp.where(sub8 == 0, pltpu.roll(x, 4, 0), pltpu.roll(x, 3, 0)),
                    jnp.where(sub8 == 0, (128 - lane8) & 63, (191 - lane8) & 127),
                )
                head = jnp.where((sub8 == 0) & (lane8 >= 64), two, x)
                tail = jnp.where((sub8 == 7) & (lane8 >= 64), two, one)
                power[8 * p : 8 * p + 8, :] = jnp.where(sub8 < 4, head, tail)

        @pl.when(cls != 0)
        def _():
            for p in range(8):
                x = power[8 * p : 8 * p + 8, :]
                power[8 * p : 8 * p + 8, :] = jnp.where(sub8 < 4, x, lanes_at(x, 127 - lane8))

        for n in range(8):
            rows_a[trial, 8 * n : 8 * n + 8, :] = power[pl.ds(n, 8, stride=8), :]

    def residue(sign):
        return cls if sign == 0 else (SLOTS - cls) & (SLOTS - 1)

    class_of = jnp.where(sub8 < 4, cls, (SLOTS - cls) & (SLOTS - 1)) + 64 * jnp.where(
        sub8 < 4, sub8, 11 - sub8
    )

    def select(trial, m, odd, shift, half):
        k1 = (INVERSE[odd] * (class_of >> shift)) & ((FIRST >> shift) - 1)
        index = ((m * k1) >> 9) + odd * (128 * half + lane8)
        total = jnp.zeros((8, 128), f32)
        for p in range(odd * half, odd * half + odd):
            total = jnp.where(
                (index >> 7) == p,
                lanes_at(powers[trial, 8 * p : 8 * p + 8, :], index & 127),
                total,
            )
        return total

    started = []

    def share(trial):
        power, by_row, term = powers.at[trial], rows_a.at[trial], terms.at[trial]
        number = [0]

        def give(source, start, m, sign, rows, to, condition):
            base = BASES[m] + (0 if m == 8 else rows * sign)
            from_ref = source.at[pl.ds(start, rows)]
            to_ref = received.at[trial, pl.ds(base, rows)]
            copy = pltpu.make_async_remote_copy(
                src_ref=from_ref, dst_ref=to_ref,
                send_sem=term_send.at[trial, number[0]], recv_sem=term_recv.at[trial],
                device_id={"fft": to}, device_id_type=mesh_id,
            )
            number[0] += 1
            away = condition & (to != me)

            @pl.when(away)
            def _():
                copy.start()

            @pl.when(condition & (to == me))
            def _():
                pltpu.make_async_copy(from_ref, to_ref, term_recv.at[trial]).start()

            started.append((copy, away))

        always, even = me >= 0, (cls & 1) == 0
        for sign in range(2):
            rest = residue(sign)
            give(power, 0, 1, sign, 8, rest, always)
            for v in range(2):
                give(power, 0, 2, sign, 16, ((rest >> 1) + 32 * v) & 63, even)
            for i in range(4):
                place = i if sign == 0 else 7 - i
                at = 32 * sign + 8 * i
                give(by_row, at, 4, sign, 8, ((rest >> 2) + 16 * place) & 63, (cls & 3) == 0)
                give(by_row, at, 8, sign, 8, ((rest >> 3) + 8 * place) & 63, (cls & 7) == 0)
        for n, m in enumerate((3, 5, 7)):
            term[8 * n : 8 * n + 8, :] = select(trial, m, m, 0, 0)
            for sign in range(2):
                give(term, 8 * n, m, sign, 8, (INVERSE[m] * residue(sign)) & 63, always)
        for half in range(2):
            term[24 + 8 * half : 32 + 8 * half, :] = select(trial, 6, 3, 1, half)
        for sign in range(2):
            for v in range(2):
                to = (INVERSE[3] * ((residue(sign) >> 1) + 32 * v)) & 63
                give(term, 24, 6, sign, 16, to, even)

    def source_row(m, v, rows):
        place = (((m * me) >> 6) + m * v) & 7
        sign = place >> 2
        slot = jnp.where(sign == 1, 7 - place, place)
        return BASES[m] + (rows + 4) * sign + slot

    def collect(trial):
        def row_at(index):
            return received[trial, pl.ds(index, 1), :]

        total = received[trial, pl.ds(BASES[8], 8), :]
        for v in range(2):
            base = BASES[4] + 8 * v
            values = jnp.broadcast_to(row_at(base), (8, 128))
            for p in range(1, 4):
                values = jnp.where((sub8 >> 1) == p, row_at(base + p), values)
            values = lanes_at(values, 64 * (sub8 & 1) + (lane8 >> 1))
            total = total + jnp.where((lane8 & 1) == v, values, 0.0)
        for v in range(4):
            at2, at6 = source_row(2, v, 16), source_row(6, v, 16)
            low = row_at(at2) + row_at(at6)
            high = row_at(at2 + 8) + row_at(at6 + 8)
            values = jnp.where((sub8 >> 2) == 0, low, high)
            values = lanes_at(values, 32 * (sub8 & 3) + (lane8 >> 2))
            total = total + jnp.where((lane8 & 3) == v, values, 0.0)
        for v in range(8):
            values = row_at(source_row(1, v, 8))
            for m in (3, 5, 7):
                values = values + row_at(source_row(m, v, 8))
            values = lanes_at(jnp.broadcast_to(values, (8, 128)), 16 * sub8 + (lane8 >> 3))
            total = total + jnp.where((lane8 & 7) == v, values, 0.0)
        out[trial] = total * (0.125 / LENGTH)

    for trial in range(2):
        arrived(recv1.at[trial], recv1_sem.at[trial])
        if trial == 0:
            arrived(fixed.at[pl.ds(0, SLOTS)], fix_sem.at[1])
            right = fixed[pl.ds(0, 64, stride=8), :]
            for rg, at in ((0, 0), (7, 127)):
                where = pl.ds(rg, 64, stride=8)
                recv1[0, where, :] = jnp.where(lane64 == at, right, recv1[0, where, :])
        transform(trial)
        exchange(
            send2.at[trial], recv2.at[trial], send2_sem.at[trial], recv2_sem.at[trial],
            block_of=class_at,
        )
    for trial in range(2):
        arrived(recv2.at[trial], recv2_sem.at[trial])
        finish(trial)
        share(trial)
    arrived(received.at[0], term_recv.at[0])
    collect(0)

    @pl.when(me < SLOTS - 1)
    def _():
        to_next.wait_send()

    @pl.when(me > 0)
    def _():
        to_last.wait_send()

    sent(fixes, fix_sem.at[0], 1)
    for trial in range(2):
        sent(send1.at[trial], send1_sem.at[trial])
        sent(send2.at[trial], send2_sem.at[trial])
    for copy, away in started:

        @pl.when(away)
        def _(copy=copy):
            copy.wait_send()

    arrived(received.at[1], term_recv.at[1])
    collect(1)


def on_device(series, filters, delays, phases):
    tables = [jnp.asarray(table) for table in make_tables()]
    whole = pl.BlockSpec(memory_space=pltpu.VMEM)
    anywhere = pl.BlockSpec(memory_space=pl.ANY)
    f32 = jnp.float32
    out = pl.pallas_call(
        kernel,
        out_shape=jax.ShapeDtypeStruct((2, 8, 128), f32),
        in_specs=[anywhere] * (4 + len(tables)),
        out_specs=whole,
        scratch_shapes=[
            pltpu.VMEM((2, 16), jnp.int32),
            pltpu.VMEM((2, 16), jnp.int32),
            pltpu.VMEM((TAPS, PHASES), f32),
            pltpu.VMEM((528, 128), f32),
            pltpu.VMEM((2, 8, 128), f32),
            pltpu.VMEM((512, 128), f32),
            pltpu.VMEM((512, 128), f32),
            pltpu.VMEM((32, 256), f32),
            pltpu.VMEM((8, 256, 128), jnp.bfloat16),
            pltpu.VMEM((8, 256, 128), jnp.bfloat16),
            pltpu.VMEM((2, 512, 128), f32),
            pltpu.VMEM((2, 512, 128), f32),
            pltpu.VMEM((2, 512, 128), f32),
            pltpu.VMEM((2, 512, 128), f32),
            pltpu.VMEM((2 * FREQS, 128), f32),
            pltpu.VMEM((2, FREQS, 128), f32),
            pltpu.VMEM((2, 64, 128), f32),
            pltpu.VMEM((2, 64, 128), f32),
            pltpu.VMEM((2, 40, 128), f32),
            pltpu.VMEM((2, TERM_ROWS, 128), f32),
        ]
        + [pltpu.VMEM(table.shape, table.dtype) for table in tables]
        + [
            pltpu.SemaphoreType.DMA((3,)),
            pltpu.SemaphoreType.DMA((len(tables),)),
            pltpu.SemaphoreType.DMA,
            pltpu.SemaphoreType.DMA((2,)),
            pltpu.SemaphoreType.DMA((2,)),
            pltpu.SemaphoreType.DMA((2,)),
            pltpu.SemaphoreType.DMA((2,)),
            pltpu.SemaphoreType.DMA((2,)),
            pltpu.SemaphoreType.DMA((2,)),
            pltpu.SemaphoreType.DMA((2,)),
            pltpu.SemaphoreType.DMA((2, 32)),
            pltpu.SemaphoreType.DMA((2,)),
        ],
        compiler_params=pltpu.CompilerParams(
            collective_id=0, has_side_effects=True
        ),
    )(series.reshape(512, 128), delays, phases, filters.T, *tables)
    return out.reshape(2, 1, 1024)


def solution(mesh):
    return jax.shard_map(
        on_device,
        mesh=mesh,
        in_specs=(P(("dm", "fft")), P(), P(None, "fft"), P(None, "fft")),
        out_specs=P("dm", "fft", None),
        check_vma=False,
    )
```

```python
import jax
import jax.numpy as jnp
import ml_dtypes
import numpy as np
from jax import lax
from jax.experimental import pallas as pl
from jax.experimental.pallas import tpu as pltpu
from jax.sharding import PartitionSpec as P

LENGTH = 4194304
SLOTS = 64
TAPS = 16
PHASES = 32
FIRST = 512
SECOND = 128
FREQS = 272
INVERSE = {1: 1, 3: 171, 5: 205, 7: 439}
BASES = {1: 0, 3: 16, 5: 32, 7: 48, 2: 64, 6: 96, 4: 128, 8: 144}
TERM_ROWS = 152
PAIRS = (
    6, 16, 3, 24, 18, 22, 2, 15, 5, 4, 21, 12, 28, 17, 31, 8,
    7, 9, 20, 19, 25, 11, 13, 26, 0, 30, 14, 10, 23, 29, 27, 1,
)


def split_table(table):
    table = np.asarray(table, np.float32)
    high = table.astype(ml_dtypes.bfloat16)
    low = (table - high.astype(np.float32)).astype(ml_dtypes.bfloat16)
    return high, low


def make_tables():
    turn = 2.0 * np.pi
    angle = turn / FIRST * (np.arange(FREQS)[:, None] * np.arange(FIRST)[None, :] % FIRST)
    first = np.concatenate([np.cos(angle), -np.sin(angle)], axis=0)
    h, rr, c_hi = np.meshgrid(np.arange(2), np.arange(2), np.arange(32), indexing="ij")
    second_index = (64 * rr + 2 * c_hi + h).reshape(-1)
    angle = turn / 65536 * (np.arange(FREQS)[:, None] * second_index[None, :] % 65536)
    mid = np.stack([np.cos(angle), -np.sin(angle)]).astype(np.float32)
    angle = turn / SECOND * (second_index[:, None] * np.arange(SECOND)[None, :] % SECOND)
    cos_part, sin_part = np.cos(angle), np.sin(angle)
    second = np.block([[cos_part, -sin_part], [sin_part, cos_part]])
    angle = turn / LENGTH * (np.arange(FREQS)[:, None] * np.arange(128)[None, :])
    col = np.stack([np.cos(angle), -np.sin(angle)]).astype(np.float32)
    angle = turn / 8192 * (np.arange(SLOTS)[:, None] * np.arange(SECOND)[None, :] % 8192)
    row = np.stack([np.cos(angle), -np.sin(angle)]).astype(np.float32)
    last = np.zeros((2, 8, 2, 4, SLOTS, 4, 2))
    special = np.zeros((2, 2, 8, SLOTS, 4, 2))
    q = np.arange(SLOTS)
    for sign in range(2):
        for p in range(8):
            actual = p if sign == 0 else -1 - p
            theta = turn / 64 * (q * actual % 64)
            for i in range(4):
                last[0, p, sign, i, :, i, 0] = np.cos(theta)
                last[0, p, sign, i, :, i, 1] = np.sin(theta)
                last[1, p, sign, i, :, i, 0] = -np.sin(theta)
                last[1, p, sign, i, :, i, 1] = np.cos(theta)
            theta = turn / 128 * (q * (2 * p + sign) % 128)
            special[0, sign, p, :, 0, sign] = np.cos(theta)
            special[1, sign, p, :, 0, sign] = -np.sin(theta)
    last = np.concatenate([last.reshape(128, 512), special.reshape(32, 512)], axis=0)
    return (*split_table(first), *split_table(second), *split_table(last), mid, col, row)


def split(x):
    high = x.astype(jnp.bfloat16)
    return high, (x - high.astype(jnp.float32)).astype(jnp.bfloat16)


def dot(a, b):
    return jnp.dot(a, b, preferred_element_type=jnp.float32)


def product(a_high, a_low, b_high, b_low):
    wide = dot(a_high, jnp.concatenate([b_high, b_low], 1))
    return wide[:, 0:128] + wide[:, 128:256] + dot(a_low, b_high)


def lanes_at(x, index):
    return jnp.take_along_axis(x, index, axis=1, mode="promise_in_bounds")


def iota(shape, axis):
    return lax.broadcasted_iota(jnp.int32, shape, axis)


def class_at(device):
    words = [sum(PAIRS[4 * n + b] << (8 * b) for b in range(4)) for n in range(8)]
    chip = device >> 1
    word = jnp.int32(words[0])
    for n in range(1, 8):
        word = jnp.where((chip >> 2) == n, jnp.int32(words[n]), word)
    pair = (word >> ((chip & 3) << 3)) & 31
    other = jnp.where(pair == 0, SLOTS // 2, SLOTS - pair)
    return jnp.where((device & 1) == 0, pair, other)


def column_of(values, own, second_trial):
    chosen = jnp.where(second_trial, values[1:2, :], values[0:1, :])
    return jnp.sum(jnp.where(own, chosen, 0.0), axis=1, keepdims=True)


def kernel(
    series, delays, phases, filters,
    first_high, first_low, second_high, second_low, last_high, last_low, mid, col, row,
    out,
    v_delays, v_phases, v_filters, ext, halos, fixes, fixed, responses, windows_high, windows_low, send1, recv1, send2, recv2, spectrum, turn,
    powers, rows_a, terms, received,
    v_first_high, v_first_low, v_second_high, v_second_low, v_last_high, v_last_low,
    v_mid, v_col, v_row,
    small_sem, table_sem, series_sem, halo_send, halo_recv, fix_sem,
    send1_sem, recv1_sem, send2_sem, recv2_sem, term_send, term_recv,
):
    me = lax.axis_index("fft")
    cls = class_at(me)
    f32 = jnp.float32
    mesh_id = pl.DeviceIdType.MESH

    barrier = pltpu.get_barrier_semaphore()

    def partner(act, dz, dy, dc):
        y, z = ((me >> 4) + dy) & 3, ((me >> 1) + dz) & 7
        act((y << 4) + (z << 1) + ((me & 1) ^ dc))

    def same_z(act):
        for dy in (2, 1, 3, 0):
            for dc in range(2):
                if dy or dc:
                    partner(act, 0, dy, dc)

    def partners(act):
        def block(step, carry):
            dy = (0x36 >> (step & 6)) & 3
            for dz in (3, 5, 4, 2, 6, 1, 7):
                partner(act, dz, dy, step & 1)
            return carry

        lax.fori_loop(0, 8, block, 0)
        same_z(act)

    def far_first(act):
        def ring(step, carry):
            dz = (0x7162534 >> (4 * step)) & 7
            for dy in (2, 1, 3, 0):
                for dc in range(2):
                    partner(act, dz, dy, dc)
            return carry

        lax.fori_loop(0, 7, ring, 0)
        same_z(act)

    def greet(to):
        pl.semaphore_signal(barrier, inc=1, device_id={"fft": to}, device_id_type=mesh_id)

    small = [
        pltpu.make_async_copy(source, target, small_sem.at[n])
        for n, (source, target) in enumerate(
            ((delays, v_delays), (phases, v_phases), (filters, v_filters))
        )
    ]
    for copy in small:
        copy.start()
    own_series = pltpu.make_async_copy(series, ext.at[pl.ds(8, 512)], series_sem)
    own_series.start()
    far_first(greet)
    tables = [
        pltpu.make_async_copy(source, target, table_sem.at[n])
        for n, (source, target) in enumerate(
            (
                (first_high, v_first_high), (first_low, v_first_low),
                (second_high, v_second_high), (second_low, v_second_low),
                (last_high, v_last_high), (last_low, v_last_low),
                (mid, v_mid), (col, v_col), (row, v_row),
            )
        )
    ]

    for copy in small:
        copy.wait()
    line = iota((32, 16), 0)
    own = iota((32, 16), 1) == 2 * (line >> 2) + (line & 1)
    second_trial = ((line >> 1) & 1) == 1
    delay = column_of(v_delays[...].astype(f32), own, second_trial)
    phase = column_of(v_phases[...].astype(f32), own, second_trial)
    branch = (iota((32, PHASES), 1).astype(f32) == phase).astype(f32)
    taps = lax.dot_general(
        branch, v_filters[...], (((1,), (1,)), ((), ())),
        precision=lax.Precision.HIGHEST, preferred_element_type=f32,
    )
    position = iota((32, 256), 1).astype(f32) - (delay + 56.0)
    response = jnp.zeros((32, 256), f32)
    for tap in range(TAPS):
        response = jnp.where(position == float(tap), taps[:, tap : tap + 1], response)
    responses[...] = response

    own_series.wait()
    ext[0:8, :] = jnp.zeros((8, 128), f32)
    ext[520:528, :] = jnp.zeros((8, 128), f32)

    lane64 = iota((64, 128), 1)

    def resample(trial, rg):
        if trial == 0:
            before = ext[pl.ds(64 * rg + 7, 64), :]
            here = ext[pl.ds(64 * rg + 8, 64), :]
            after = ext[pl.ds(64 * rg + 9, 64), :]
            left = pltpu.roll(jnp.where(lane64 < 64, here, before), 64, 1)
            right = pltpu.roll(jnp.where(lane64 < 64, after, here), 64, 1)
            window = jnp.concatenate(
                [jnp.concatenate([left, here], 0).T, jnp.concatenate([right, after], 0).T], 0
            )
            w_high, w_low = split(window)
            windows_high[rg], windows_low[rg] = w_high, w_low
        else:
            w_high, w_low = windows_high[rg], windows_low[rg]
        bands = []
        for rr in range(2):
            line = responses[pl.ds(4 * rg + 2 * trial + rr, 1), :]
            bands.append(
                pltpu.roll(jnp.broadcast_to(line, (64, 256)), 0, 1, stride=1, stride_axis=0)
            )
        b_high, b_low = split(jnp.concatenate(bands, 0))
        both = product(b_high, b_low, w_high, w_low)
        return jnp.where((lane64 & 32) == 0, both[0:64], both[64:128])

    def exchange(source, target, send_sem, recv_sem, rows=8, block_of=lambda device: device):
        mine = pl.ds(pl.multiple_of(8 * me, 8), rows)

        def block(device):
            return source.at[pl.ds(pl.multiple_of(8 * block_of(device), 8), rows)]

        def send(to):
            pltpu.make_async_remote_copy(
                src_ref=block(to), dst_ref=target.at[mine],
                send_sem=send_sem, recv_sem=recv_sem,
                device_id={"fft": to}, device_id_type=mesh_id,
            ).start()

        partners(send)
        pltpu.make_async_copy(block(me), target.at[mine], recv_sem).start()

    def arrived(target, sem):
        pltpu.make_async_copy(target, target, sem).wait()

    def sent(source, sem, rows=8):
        part = source.at[pl.ds(0, rows * (SLOTS - 1))]
        pltpu.make_async_copy(part, part, sem).wait()

    def inner(trial):
        def body(rg, carry):
            send1[trial, pl.ds(rg, 64, stride=8), :] = resample(trial, rg)
            return carry

        return body

    lax.fori_loop(0, 8, inner(0), 0)
    pl.semaphore_wait(barrier, SLOTS - 1)
    to_next = pltpu.make_async_remote_copy(
        src_ref=series.at[pl.ds(504, 8)], dst_ref=halos.at[0],
        send_sem=halo_send.at[0], recv_sem=halo_recv.at[0],
        device_id={"fft": (me + 1) & (SLOTS - 1)}, device_id_type=mesh_id,
    )
    to_last = pltpu.make_async_remote_copy(
        src_ref=series.at[pl.ds(0, 8)], dst_ref=halos.at[1],
        send_sem=halo_send.at[1], recv_sem=halo_recv.at[1],
        device_id={"fft": (me + SLOTS - 1) & (SLOTS - 1)}, device_id_type=mesh_id,
    )

    @pl.when(me < SLOTS - 1)
    def _():
        to_next.start()

    @pl.when(me > 0)
    def _():
        to_last.start()

    exchange(send1.at[0], recv1.at[0], send1_sem.at[0], recv1_sem.at[0])
    for copy in tables:
        copy.start()
    lax.fori_loop(1, 7, inner(1), 0)

    @pl.when(me > 0)
    def _():
        to_next.wait_recv()
        ext[0:8, :] = halos[0]

    @pl.when(me < SLOTS - 1)
    def _():
        to_last.wait_recv()
        ext[520:528, :] = halos[1]

    def fix(end, held):
        return jnp.where(lane64 >= 64 * end, resample(0, 7 * end), held)

    fixes[pl.ds(0, 64, stride=8), :] = lax.fori_loop(0, 2, fix, jnp.zeros((64, 128), f32))
    exchange(fixes, fixed, fix_sem.at[0], fix_sem.at[1], 1)
    lax.fori_loop(0, 2, lambda end, carry: inner(1)(7 * end, carry), 0)
    exchange(send1.at[1], recv1.at[1], send1_sem.at[1], recv1_sem.at[1])

    for copy in tables:
        copy.wait()
    me_lane = iota((FREQS, 128), 1) == me
    col_cos = jnp.sum(jnp.where(me_lane, v_col[0], 0.0), axis=1, keepdims=True)
    col_sin = jnp.sum(jnp.where(me_lane, v_col[1], 0.0), axis=1, keepdims=True)
    row_cos = v_row[0, pl.ds(me, 1), :]
    row_sin = v_row[1, pl.ds(me, 1), :]
    turn[0] = col_cos * row_cos - col_sin * row_sin
    turn[1] = col_cos * row_sin + col_sin * row_cos
    lane1 = iota((1, 128), 1)
    lane8, sub8 = iota((8, 128), 1), iota((8, 128), 0)

    def transform(trial):
        d_high, d_low = split(recv1[trial])
        spectrum[...] = product(v_first_high[...], v_first_low[...], d_high, d_low)
        real, imaginary = spectrum[0:FREQS, :], spectrum[FREQS : 2 * FREQS, :]
        mid_cos, mid_sin = v_mid[0], v_mid[1]
        turned = jnp.concatenate(
            [real * mid_cos - imaginary * mid_sin, real * mid_sin + imaginary * mid_cos], 1
        )
        t_high, t_low = split(turned)
        s_high = v_second_high[...]
        result = dot(t_high, s_high) + dot(t_low, s_high) + dot(t_high, v_second_low[...])
        real, imaginary = result[:, 0:128], result[:, 128:256]
        turn_cos, turn_sin = turn[0], turn[1]
        parts = (
            real * turn_cos - imaginary * turn_sin,
            real * turn_sin + imaginary * turn_cos,
        )
        middle = pltpu.roll(real[0:1], 64, 1)
        for c in range(2):
            for i in range(4):
                send2[trial, pl.ds(2 * i + c, 64, stride=8), :] = parts[c][64 * i : 64 * i + 64]
            packed = jnp.where(lane1 < 64, parts[c][0:1], pltpu.roll(parts[c][256:257], 64, 1))
            if c == 1:
                packed = jnp.where(lane1 == 0, middle, packed)
            send2[trial, c : c + 1, :] = packed

    def finish(trial):
        r_high, r_low = split(recv2[trial])
        final = product(v_last_high[...], v_last_low[...], r_high, r_low)
        power = powers.at[trial]
        power[...] = final[0:64] ** 2 + final[64:128] ** 2
        special = final[128:144] ** 2 + final[144:160] ** 2

        @pl.when(cls == 0)
        def _():
            for sign in range(2):
                where = pl.ds(4 * sign, 8, stride=8)
                power[where, :] = jnp.where(
                    lane8 == 0, special[8 * sign : 8 * sign + 8], power[where, :]
                )
            for p in range(8):
                x = power[8 * p : 8 * p + 8, :]
                one = lanes_at(
                    pltpu.roll(x, 7, 0), jnp.where(sub8 == 7, lane8 + 64, 127 - lane8) & 127
                )
                two = lanes_at(
                    jnp.where(sub8 == 0, pltpu.roll(x, 4, 0), pltpu.roll(x, 3, 0)),
                    jnp.where(sub8 == 0, (128 - lane8) & 63, (191 - lane8) & 127),
                )
                head = jnp.where((sub8 == 0) & (lane8 >= 64), two, x)
                tail = jnp.where((sub8 == 7) & (lane8 >= 64), two, one)
                power[8 * p : 8 * p + 8, :] = jnp.where(sub8 < 4, head, tail)

        @pl.when(cls != 0)
        def _():
            for p in range(8):
                x = power[8 * p : 8 * p + 8, :]
                power[8 * p : 8 * p + 8, :] = jnp.where(sub8 < 4, x, lanes_at(x, 127 - lane8))

        for n in range(8):
            rows_a[trial, 8 * n : 8 * n + 8, :] = power[pl.ds(n, 8, stride=8), :]

    def residue(sign):
        return cls if sign == 0 else (SLOTS - cls) & (SLOTS - 1)

    class_of = jnp.where(sub8 < 4, cls, (SLOTS - cls) & (SLOTS - 1)) + 64 * jnp.where(
        sub8 < 4, sub8, 11 - sub8
    )

    def select(trial, m, odd, shift, half):
        k1 = (INVERSE[odd] * (class_of >> shift)) & ((FIRST >> shift) - 1)
        index = ((m * k1) >> 9) + odd * (128 * half + lane8)
        total = jnp.zeros((8, 128), f32)
        for p in range(odd * half, odd * half + odd):
            total = jnp.where(
                (index >> 7) == p,
                lanes_at(powers[trial, 8 * p : 8 * p + 8, :], index & 127),
                total,
            )
        return total

    started = []

    def share(trial):
        power, by_row, term = powers.at[trial], rows_a.at[trial], terms.at[trial]
        number = [0]

        def give(source, start, m, sign, rows, to, condition):
            base = BASES[m] + (0 if m == 8 else rows * sign)
            from_ref = source.at[pl.ds(start, rows)]
            to_ref = received.at[trial, pl.ds(base, rows)]
            copy = pltpu.make_async_remote_copy(
                src_ref=from_ref, dst_ref=to_ref,
                send_sem=term_send.at[trial, number[0]], recv_sem=term_recv.at[trial],
                device_id={"fft": to}, device_id_type=mesh_id,
            )
            number[0] += 1
            away = condition & (to != me)

            @pl.when(away)
            def _():
                copy.start()

            @pl.when(condition & (to == me))
            def _():
                pltpu.make_async_copy(from_ref, to_ref, term_recv.at[trial]).start()

            started.append((copy, away))

        always, even = me >= 0, (cls & 1) == 0
        for sign in range(2):
            rest = residue(sign)
            give(power, 0, 1, sign, 8, rest, always)
            for v in range(2):
                give(power, 0, 2, sign, 16, ((rest >> 1) + 32 * v) & 63, even)
            for i in range(4):
                place = i if sign == 0 else 7 - i
                at = 32 * sign + 8 * i
                give(by_row, at, 4, sign, 8, ((rest >> 2) + 16 * place) & 63, (cls & 3) == 0)
                give(by_row, at, 8, sign, 8, ((rest >> 3) + 8 * place) & 63, (cls & 7) == 0)
        for n, m in enumerate((3, 5, 7)):
            term[8 * n : 8 * n + 8, :] = select(trial, m, m, 0, 0)
            for sign in range(2):
                give(term, 8 * n, m, sign, 8, (INVERSE[m] * residue(sign)) & 63, always)
        for half in range(2):
            term[24 + 8 * half : 32 + 8 * half, :] = select(trial, 6, 3, 1, half)
        for sign in range(2):
            for v in range(2):
                to = (INVERSE[3] * ((residue(sign) >> 1) + 32 * v)) & 63
                give(term, 24, 6, sign, 16, to, even)

    def source_row(m, v, rows):
        place = (((m * me) >> 6) + m * v) & 7
        sign = place >> 2
        slot = jnp.where(sign == 1, 7 - place, place)
        return BASES[m] + (rows + 4) * sign + slot

    def collect(trial):
        def row_at(index):
            return received[trial, pl.ds(index, 1), :]

        total = received[trial, pl.ds(BASES[8], 8), :]
        for v in range(2):
            base = BASES[4] + 8 * v
            values = jnp.broadcast_to(row_at(base), (8, 128))
            for p in range(1, 4):
                values = jnp.where((sub8 >> 1) == p, row_at(base + p), values)
            values = lanes_at(values, 64 * (sub8 & 1) + (lane8 >> 1))
            total = total + jnp.where((lane8 & 1) == v, values, 0.0)
        for v in range(4):
            at2, at6 = source_row(2, v, 16), source_row(6, v, 16)
            low = row_at(at2) + row_at(at6)
            high = row_at(at2 + 8) + row_at(at6 + 8)
            values = jnp.where((sub8 >> 2) == 0, low, high)
            values = lanes_at(values, 32 * (sub8 & 3) + (lane8 >> 2))
            total = total + jnp.where((lane8 & 3) == v, values, 0.0)
        for v in range(8):
            values = row_at(source_row(1, v, 8))
            for m in (3, 5, 7):
                values = values + row_at(source_row(m, v, 8))
            values = lanes_at(jnp.broadcast_to(values, (8, 128)), 16 * sub8 + (lane8 >> 3))
            total = total + jnp.where((lane8 & 7) == v, values, 0.0)
        out[trial] = total * (0.125 / LENGTH)

    for trial in range(2):
        arrived(recv1.at[trial], recv1_sem.at[trial])
        if trial == 0:
            arrived(fixed.at[pl.ds(0, SLOTS)], fix_sem.at[1])
            right = fixed[pl.ds(0, 64, stride=8), :]
            for rg, at in ((0, 0), (7, 127)):
                where = pl.ds(rg, 64, stride=8)
                recv1[0, where, :] = jnp.where(lane64 == at, right, recv1[0, where, :])
        transform(trial)
        exchange(
            send2.at[trial], recv2.at[trial], send2_sem.at[trial], recv2_sem.at[trial],
            block_of=class_at,
        )
    for trial in range(2):
        arrived(recv2.at[trial], recv2_sem.at[trial])
        finish(trial)
        share(trial)
    arrived(received.at[0], term_recv.at[0])
    collect(0)

    @pl.when(me < SLOTS - 1)
    def _():
        to_next.wait_send()

    @pl.when(me > 0)
    def _():
        to_last.wait_send()

    sent(fixes, fix_sem.at[0], 1)
    for trial in range(2):
        sent(send1.at[trial], send1_sem.at[trial])
        sent(send2.at[trial], send2_sem.at[trial])
    for copy, away in started:

        @pl.when(away)
        def _(copy=copy):
            copy.wait_send()

    arrived(received.at[1], term_recv.at[1])
    collect(1)


def on_device(series, filters, delays, phases):
    tables = [jnp.asarray(table) for table in make_tables()]
    whole = pl.BlockSpec(memory_space=pltpu.VMEM)
    anywhere = pl.BlockSpec(memory_space=pl.ANY)
    f32 = jnp.float32
    out = pl.pallas_call(
        kernel,
        out_shape=jax.ShapeDtypeStruct((2, 8, 128), f32),
        in_specs=[anywhere] * (4 + len(tables)),
        out_specs=whole,
        scratch_shapes=[
            pltpu.VMEM((2, 16), jnp.int32),
            pltpu.VMEM((2, 16), jnp.int32),
            pltpu.VMEM((TAPS, PHASES), f32),
            pltpu.VMEM((528, 128), f32),
            pltpu.VMEM((2, 8, 128), f32),
            pltpu.VMEM((512, 128), f32),
            pltpu.VMEM((512, 128), f32),
            pltpu.VMEM((32, 256), f32),
            pltpu.VMEM((8, 256, 128), jnp.bfloat16),
            pltpu.VMEM((8, 256, 128), jnp.bfloat16),
            pltpu.VMEM((2, 512, 128), f32),
            pltpu.VMEM((2, 512, 128), f32),
            pltpu.VMEM((2, 512, 128), f32),
            pltpu.VMEM((2, 512, 128), f32),
            pltpu.VMEM((2 * FREQS, 128), f32),
            pltpu.VMEM((2, FREQS, 128), f32),
            pltpu.VMEM((2, 64, 128), f32),
            pltpu.VMEM((2, 64, 128), f32),
            pltpu.VMEM((2, 40, 128), f32),
            pltpu.VMEM((2, TERM_ROWS, 128), f32),
        ]
        + [pltpu.VMEM(table.shape, table.dtype) for table in tables]
        + [
            pltpu.SemaphoreType.DMA((3,)),
            pltpu.SemaphoreType.DMA((len(tables),)),
            pltpu.SemaphoreType.DMA,
            pltpu.SemaphoreType.DMA((2,)),
            pltpu.SemaphoreType.DMA((2,)),
            pltpu.SemaphoreType.DMA((2,)),
            pltpu.SemaphoreType.DMA((2,)),
            pltpu.SemaphoreType.DMA((2,)),
            pltpu.SemaphoreType.DMA((2,)),
            pltpu.SemaphoreType.DMA((2,)),
            pltpu.SemaphoreType.DMA((2, 32)),
            pltpu.SemaphoreType.DMA((2,)),
        ],
        compiler_params=pltpu.CompilerParams(
            collective_id=0, has_side_effects=True
        ),
    )(series.reshape(512, 128), delays, phases, filters.T, *tables)
    return out.reshape(2, 1, 1024)


def solution(mesh):
    return jax.shard_map(
        on_device,
        mesh=mesh,
        in_specs=(P(("dm", "fft")), P(), P(None, "fft"), P(None, "fft")),
        out_specs=P("dm", "fft", None),
        check_vma=False,
    )
```

```python
import jax
import jax.numpy as jnp
import ml_dtypes
import numpy as np
from jax import lax
from jax.experimental import pallas as pl
from jax.experimental.pallas import tpu as pltpu
from jax.sharding import PartitionSpec as P

LENGTH = 4194304
SLOTS = 64
TAPS = 16
PHASES = 32
FIRST = 512
SECOND = 128
FREQS = 272
INVERSE = {1: 1, 3: 171, 5: 205, 7: 439}
BASES = {1: 0, 3: 16, 5: 32, 7: 48, 2: 64, 6: 96, 4: 128, 8: 144}
TERM_ROWS = 152
PAIRS = (
    6, 16, 3, 24, 18, 22, 2, 15, 5, 4, 21, 12, 28, 17, 31, 8,
    7, 9, 20, 19, 25, 11, 13, 26, 0, 30, 14, 10, 23, 29, 27, 1,
)


def split_table(table):
    table = np.asarray(table, np.float32)
    high = table.astype(ml_dtypes.bfloat16)
    low = (table - high.astype(np.float32)).astype(ml_dtypes.bfloat16)
    return high, low


def make_tables():
    turn = 2.0 * np.pi
    angle = turn / FIRST * (np.arange(FREQS)[:, None] * np.arange(FIRST)[None, :] % FIRST)
    first = np.concatenate([np.cos(angle), -np.sin(angle)], axis=0)
    h, rr, c_hi = np.meshgrid(np.arange(2), np.arange(2), np.arange(32), indexing="ij")
    second_index = (64 * rr + 2 * c_hi + h).reshape(-1)
    angle = turn / 65536 * (np.arange(FREQS)[:, None] * second_index[None, :] % 65536)
    mid = np.stack([np.cos(angle), -np.sin(angle)]).astype(np.float32)
    angle = turn / SECOND * (second_index[:, None] * np.arange(SECOND)[None, :] % SECOND)
    cos_part, sin_part = np.cos(angle), np.sin(angle)
    second = np.block([[cos_part, -sin_part], [sin_part, cos_part]])
    angle = turn / LENGTH * (np.arange(FREQS)[:, None] * np.arange(128)[None, :])
    col = np.stack([np.cos(angle), -np.sin(angle)]).astype(np.float32)
    angle = turn / 8192 * (np.arange(SLOTS)[:, None] * np.arange(SECOND)[None, :] % 8192)
    row = np.stack([np.cos(angle), -np.sin(angle)]).astype(np.float32)
    last = np.zeros((2, 8, 2, 4, SLOTS, 4, 2))
    special = np.zeros((2, 2, 8, SLOTS, 4, 2))
    q = np.arange(SLOTS)
    for sign in range(2):
        for p in range(8):
            actual = p if sign == 0 else -1 - p
            theta = turn / 64 * (q * actual % 64)
            for i in range(4):
                last[0, p, sign, i, :, i, 0] = np.cos(theta)
                last[0, p, sign, i, :, i, 1] = np.sin(theta)
                last[1, p, sign, i, :, i, 0] = -np.sin(theta)
                last[1, p, sign, i, :, i, 1] = np.cos(theta)
            theta = turn / 128 * (q * (2 * p + sign) % 128)
            special[0, sign, p, :, 0, sign] = np.cos(theta)
            special[1, sign, p, :, 0, sign] = -np.sin(theta)
    last = np.concatenate([last.reshape(128, 512), special.reshape(32, 512)], axis=0)
    return (*split_table(first), *split_table(second), *split_table(last), mid, col, row)


def split(x):
    high = x.astype(jnp.bfloat16)
    return high, (x - high.astype(jnp.float32)).astype(jnp.bfloat16)


def dot(a, b):
    return jnp.dot(a, b, preferred_element_type=jnp.float32)


def product(a_high, a_low, b_high, b_low):
    wide = dot(a_high, jnp.concatenate([b_high, b_low], 1))
    return wide[:, 0:128] + wide[:, 128:256] + dot(a_low, b_high)


def lanes_at(x, index):
    return jnp.take_along_axis(x, index, axis=1, mode="promise_in_bounds")


def iota(shape, axis):
    return lax.broadcasted_iota(jnp.int32, shape, axis)


def class_at(device):
    words = [sum(PAIRS[4 * n + b] << (8 * b) for b in range(4)) for n in range(8)]
    chip = device >> 1
    word = jnp.int32(words[0])
    for n in range(1, 8):
        word = jnp.where((chip >> 2) == n, jnp.int32(words[n]), word)
    pair = (word >> ((chip & 3) << 3)) & 31
    other = jnp.where(pair == 0, SLOTS // 2, SLOTS - pair)
    return jnp.where((device & 1) == 0, pair, other)


def column_of(values, own, second_trial):
    chosen = jnp.where(second_trial, values[1:2, :], values[0:1, :])
    return jnp.sum(jnp.where(own, chosen, 0.0), axis=1, keepdims=True)


def kernel(
    series, delays, phases, filters,
    first_high, first_low, second_high, second_low, last_high, last_low, mid, col, row,
    out,
    v_delays, v_phases, v_filters, ext, halos, fixes, fixed, responses, windows_high, windows_low, send1, recv1, send2, recv2, spectrum, turn,
    powers, rows_a, terms, received,
    v_first_high, v_first_low, v_second_high, v_second_low, v_last_high, v_last_low,
    v_mid, v_col, v_row,
    small_sem, table_sem, series_sem, halo_send, halo_recv, fix_sem,
    send1_sem, recv1_sem, send2_sem, recv2_sem, term_send, term_recv,
):
    me = lax.axis_index("fft")
    cls = class_at(me)
    f32 = jnp.float32
    mesh_id = pl.DeviceIdType.MESH

    barrier = pltpu.get_barrier_semaphore()

    def partner(act, dz, dy, dc):
        y, z = ((me >> 4) + dy) & 3, ((me >> 1) + dz) & 7
        act((y << 4) + (z << 1) + ((me & 1) ^ dc))

    def same_z(act):
        for dy in (2, 1, 3, 0):
            for dc in range(2):
                if dy or dc:
                    partner(act, 0, dy, dc)

    def partners(act):
        def block(step, carry):
            dy = (0x36 >> (step & 6)) & 3
            for dz in (3, 5, 4, 2, 6, 1, 7):
                partner(act, dz, dy, step & 1)
            return carry

        lax.fori_loop(0, 8, block, 0)
        same_z(act)

    def far_first(act):
        def ring(step, carry):
            dz = (0x7162534 >> (4 * step)) & 7
            for dy in (2, 1, 3, 0):
                for dc in range(2):
                    partner(act, dz, dy, dc)
            return carry

        lax.fori_loop(0, 7, ring, 0)
        same_z(act)

    def greet(to):
        pl.semaphore_signal(barrier, inc=1, device_id={"fft": to}, device_id_type=mesh_id)

    small = [
        pltpu.make_async_copy(source, target, small_sem.at[n])
        for n, (source, target) in enumerate(
            ((delays, v_delays), (phases, v_phases), (filters, v_filters))
        )
    ]
    for copy in small:
        copy.start()
    own_series = pltpu.make_async_copy(series, ext.at[pl.ds(8, 512)], series_sem)
    own_series.start()
    far_first(greet)
    tables = [
        pltpu.make_async_copy(source, target, table_sem.at[n])
        for n, (source, target) in enumerate(
            (
                (first_high, v_first_high), (first_low, v_first_low),
                (second_high, v_second_high), (second_low, v_second_low),
                (last_high, v_last_high), (last_low, v_last_low),
                (mid, v_mid), (col, v_col), (row, v_row),
            )
        )
    ]

    for copy in small:
        copy.wait()
    line = iota((32, 16), 0)
    own = iota((32, 16), 1) == 2 * (line >> 2) + (line & 1)
    second_trial = ((line >> 1) & 1) == 1
    delay = column_of(v_delays[...].astype(f32), own, second_trial)
    phase = column_of(v_phases[...].astype(f32), own, second_trial)
    branch = (iota((32, PHASES), 1).astype(f32) == phase).astype(f32)
    taps = lax.dot_general(
        branch, v_filters[...], (((1,), (1,)), ((), ())),
        precision=lax.Precision.HIGHEST, preferred_element_type=f32,
    )
    position = iota((32, 256), 1).astype(f32) - (delay + 56.0)
    response = jnp.zeros((32, 256), f32)
    for tap in range(TAPS):
        response = jnp.where(position == float(tap), taps[:, tap : tap + 1], response)
    responses[...] = response

    own_series.wait()
    ext[0:8, :] = jnp.zeros((8, 128), f32)
    ext[520:528, :] = jnp.zeros((8, 128), f32)

    lane64 = iota((64, 128), 1)

    def resample(trial, rg):
        if trial == 0:
            before = ext[pl.ds(64 * rg + 7, 64), :]
            here = ext[pl.ds(64 * rg + 8, 64), :]
            after = ext[pl.ds(64 * rg + 9, 64), :]
            left = pltpu.roll(jnp.where(lane64 < 64, here, before), 64, 1)
            right = pltpu.roll(jnp.where(lane64 < 64, after, here), 64, 1)
            window = jnp.concatenate(
                [jnp.concatenate([left, here], 0).T, jnp.concatenate([right, after], 0).T], 0
            )
            w_high, w_low = split(window)
            windows_high[rg], windows_low[rg] = w_high, w_low
        else:
            w_high, w_low = windows_high[rg], windows_low[rg]
        bands = []
        for rr in range(2):
            line = responses[pl.ds(4 * rg + 2 * trial + rr, 1), :]
            bands.append(
                pltpu.roll(jnp.broadcast_to(line, (64, 256)), 0, 1, stride=1, stride_axis=0)
            )
        b_high, b_low = split(jnp.concatenate(bands, 0))
        both = product(b_high, b_low, w_high, w_low)
        return jnp.where((lane64 & 32) == 0, both[0:64], both[64:128])

    def exchange(source, target, send_sem, recv_sem, rows=8, block_of=lambda device: device, order=partners):
        mine = pl.ds(pl.multiple_of(8 * me, 8), rows)

        def block(device):
            return source.at[pl.ds(pl.multiple_of(8 * block_of(device), 8), rows)]

        def send(to):
            pltpu.make_async_remote_copy(
                src_ref=block(to), dst_ref=target.at[mine],
                send_sem=send_sem, recv_sem=recv_sem,
                device_id={"fft": to}, device_id_type=mesh_id,
            ).start()

        order(send)
        pltpu.make_async_copy(block(me), target.at[mine], recv_sem).start()

    def arrived(target, sem):
        pltpu.make_async_copy(target, target, sem).wait()

    def sent(source, sem, rows=8):
        part = source.at[pl.ds(0, rows * (SLOTS - 1))]
        pltpu.make_async_copy(part, part, sem).wait()

    def inner(trial):
        def body(rg, carry):
            send1[trial, pl.ds(rg, 64, stride=8), :] = resample(trial, rg)
            return carry

        return body

    lax.fori_loop(0, 8, inner(0), 0, unroll=2)
    pl.semaphore_wait(barrier, SLOTS - 1)
    to_next = pltpu.make_async_remote_copy(
        src_ref=series.at[pl.ds(504, 8)], dst_ref=halos.at[0],
        send_sem=halo_send.at[0], recv_sem=halo_recv.at[0],
        device_id={"fft": (me + 1) & (SLOTS - 1)}, device_id_type=mesh_id,
    )
    to_last = pltpu.make_async_remote_copy(
        src_ref=series.at[pl.ds(0, 8)], dst_ref=halos.at[1],
        send_sem=halo_send.at[1], recv_sem=halo_recv.at[1],
        device_id={"fft": (me + SLOTS - 1) & (SLOTS - 1)}, device_id_type=mesh_id,
    )

    @pl.when(me < SLOTS - 1)
    def _():
        to_next.start()

    @pl.when(me > 0)
    def _():
        to_last.start()

    exchange(send1.at[0], recv1.at[0], send1_sem.at[0], recv1_sem.at[0])
    for copy in tables:
        copy.start()
    lax.fori_loop(1, 7, inner(1), 0)

    @pl.when(me > 0)
    def _():
        to_next.wait_recv()
        ext[0:8, :] = halos[0]

    @pl.when(me < SLOTS - 1)
    def _():
        to_last.wait_recv()
        ext[520:528, :] = halos[1]

    def fix(end, held):
        return jnp.where(lane64 >= 64 * end, resample(0, 7 * end), held)

    fixes[pl.ds(0, 64, stride=8), :] = lax.fori_loop(0, 2, fix, jnp.zeros((64, 128), f32))
    exchange(fixes, fixed, fix_sem.at[0], fix_sem.at[1], 1)
    lax.fori_loop(0, 2, lambda end, carry: inner(1)(7 * end, carry), 0)
    exchange(send1.at[1], recv1.at[1], send1_sem.at[1], recv1_sem.at[1])

    for copy in tables:
        copy.wait()
    me_lane = iota((FREQS, 128), 1) == me
    col_cos = jnp.sum(jnp.where(me_lane, v_col[0], 0.0), axis=1, keepdims=True)
    col_sin = jnp.sum(jnp.where(me_lane, v_col[1], 0.0), axis=1, keepdims=True)
    row_cos = v_row[0, pl.ds(me, 1), :]
    row_sin = v_row[1, pl.ds(me, 1), :]
    turn[0] = col_cos * row_cos - col_sin * row_sin
    turn[1] = col_cos * row_sin + col_sin * row_cos
    lane1 = iota((1, 128), 1)
    lane8, sub8 = iota((8, 128), 1), iota((8, 128), 0)

    def transform(trial):
        d_high, d_low = split(recv1[trial])
        spectrum[...] = product(v_first_high[...], v_first_low[...], d_high, d_low)
        real, imaginary = spectrum[0:FREQS, :], spectrum[FREQS : 2 * FREQS, :]
        mid_cos, mid_sin = v_mid[0], v_mid[1]
        turned = jnp.concatenate(
            [real * mid_cos - imaginary * mid_sin, real * mid_sin + imaginary * mid_cos], 1
        )
        t_high, t_low = split(turned)
        s_high = v_second_high[...]
        result = dot(t_high, s_high) + dot(t_low, s_high) + dot(t_high, v_second_low[...])
        real, imaginary = result[:, 0:128], result[:, 128:256]
        turn_cos, turn_sin = turn[0], turn[1]
        parts = (
            real * turn_cos - imaginary * turn_sin,
            real * turn_sin + imaginary * turn_cos,
        )
        middle = pltpu.roll(real[0:1], 64, 1)
        for c in range(2):
            for i in range(4):
                send2[trial, pl.ds(2 * i + c, 64, stride=8), :] = parts[c][64 * i : 64 * i + 64]
            packed = jnp.where(lane1 < 64, parts[c][0:1], pltpu.roll(parts[c][256:257], 64, 1))
            if c == 1:
                packed = jnp.where(lane1 == 0, middle, packed)
            send2[trial, c : c + 1, :] = packed

    def finish(trial):
        r_high, r_low = split(recv2[trial])
        final = product(v_last_high[...], v_last_low[...], r_high, r_low)
        power = powers.at[trial]
        power[...] = final[0:64] ** 2 + final[64:128] ** 2
        special = final[128:144] ** 2 + final[144:160] ** 2

        @pl.when(cls == 0)
        def _():
            for sign in range(2):
                where = pl.ds(4 * sign, 8, stride=8)
                power[where, :] = jnp.where(
                    lane8 == 0, special[8 * sign : 8 * sign + 8], power[where, :]
                )
            for p in range(8):
                x = power[8 * p : 8 * p + 8, :]
                one = lanes_at(
                    pltpu.roll(x, 7, 0), jnp.where(sub8 == 7, lane8 + 64, 127 - lane8) & 127
                )
                two = lanes_at(
                    jnp.where(sub8 == 0, pltpu.roll(x, 4, 0), pltpu.roll(x, 3, 0)),
                    jnp.where(sub8 == 0, (128 - lane8) & 63, (191 - lane8) & 127),
                )
                head = jnp.where((sub8 == 0) & (lane8 >= 64), two, x)
                tail = jnp.where((sub8 == 7) & (lane8 >= 64), two, one)
                power[8 * p : 8 * p + 8, :] = jnp.where(sub8 < 4, head, tail)

        @pl.when(cls != 0)
        def _():
            for p in range(8):
                x = power[8 * p : 8 * p + 8, :]
                power[8 * p : 8 * p + 8, :] = jnp.where(sub8 < 4, x, lanes_at(x, 127 - lane8))

        for n in range(8):
            rows_a[trial, 8 * n : 8 * n + 8, :] = power[pl.ds(n, 8, stride=8), :]

    def residue(sign):
        return cls if sign == 0 else (SLOTS - cls) & (SLOTS - 1)

    class_of = jnp.where(sub8 < 4, cls, (SLOTS - cls) & (SLOTS - 1)) + 64 * jnp.where(
        sub8 < 4, sub8, 11 - sub8
    )

    def select(trial, m, odd, shift, half):
        k1 = (INVERSE[odd] * (class_of >> shift)) & ((FIRST >> shift) - 1)
        index = ((m * k1) >> 9) + odd * (128 * half + lane8)
        total = jnp.zeros((8, 128), f32)
        for p in range(odd * half, odd * half + odd):
            total = jnp.where(
                (index >> 7) == p,
                lanes_at(powers[trial, 8 * p : 8 * p + 8, :], index & 127),
                total,
            )
        return total

    started = []

    def share(trial):
        power, by_row, term = powers.at[trial], rows_a.at[trial], terms.at[trial]
        number = [0]

        def give(source, start, m, sign, rows, to, condition):
            base = BASES[m] + (0 if m == 8 else rows * sign)
            from_ref = source.at[pl.ds(start, rows)]
            to_ref = received.at[trial, pl.ds(base, rows)]
            copy = pltpu.make_async_remote_copy(
                src_ref=from_ref, dst_ref=to_ref,
                send_sem=term_send.at[trial, number[0]], recv_sem=term_recv.at[trial],
                device_id={"fft": to}, device_id_type=mesh_id,
            )
            number[0] += 1
            away = condition & (to != me)

            @pl.when(away)
            def _():
                copy.start()

            @pl.when(condition & (to == me))
            def _():
                pltpu.make_async_copy(from_ref, to_ref, term_recv.at[trial]).start()

            started.append((copy, away))

        always, even = me >= 0, (cls & 1) == 0
        for sign in range(2):
            rest = residue(sign)
            give(power, 0, 1, sign, 8, rest, always)
            for v in range(2):
                give(power, 0, 2, sign, 16, ((rest >> 1) + 32 * v) & 63, even)
            for i in range(4):
                place = i if sign == 0 else 7 - i
                at = 32 * sign + 8 * i
                give(by_row, at, 4, sign, 8, ((rest >> 2) + 16 * place) & 63, (cls & 3) == 0)
                give(by_row, at, 8, sign, 8, ((rest >> 3) + 8 * place) & 63, (cls & 7) == 0)
        for n, m in enumerate((3, 5, 7)):
            term[8 * n : 8 * n + 8, :] = select(trial, m, m, 0, 0)
            for sign in range(2):
                give(term, 8 * n, m, sign, 8, (INVERSE[m] * residue(sign)) & 63, always)
        for half in range(2):
            term[24 + 8 * half : 32 + 8 * half, :] = select(trial, 6, 3, 1, half)
        for sign in range(2):
            for v in range(2):
                to = (INVERSE[3] * ((residue(sign) >> 1) + 32 * v)) & 63
                give(term, 24, 6, sign, 16, to, even)

    def source_row(m, v, rows):
        place = (((m * me) >> 6) + m * v) & 7
        sign = place >> 2
        slot = jnp.where(sign == 1, 7 - place, place)
        return BASES[m] + (rows + 4) * sign + slot

    def collect(trial):
        def row_at(index):
            return received[trial, pl.ds(index, 1), :]

        total = received[trial, pl.ds(BASES[8], 8), :]
        for v in range(2):
            base = BASES[4] + 8 * v
            values = jnp.broadcast_to(row_at(base), (8, 128))
            for p in range(1, 4):
                values = jnp.where((sub8 >> 1) == p, row_at(base + p), values)
            values = lanes_at(values, 64 * (sub8 & 1) + (lane8 >> 1))
            total = total + jnp.where((lane8 & 1) == v, values, 0.0)
        for v in range(4):
            at2, at6 = source_row(2, v, 16), source_row(6, v, 16)
            low = row_at(at2) + row_at(at6)
            high = row_at(at2 + 8) + row_at(at6 + 8)
            values = jnp.where((sub8 >> 2) == 0, low, high)
            values = lanes_at(values, 32 * (sub8 & 3) + (lane8 >> 2))
            total = total + jnp.where((lane8 & 3) == v, values, 0.0)
        for v in range(8):
            values = row_at(source_row(1, v, 8))
            for m in (3, 5, 7):
                values = values + row_at(source_row(m, v, 8))
            values = lanes_at(jnp.broadcast_to(values, (8, 128)), 16 * sub8 + (lane8 >> 3))
            total = total + jnp.where((lane8 & 7) == v, values, 0.0)
        out[trial] = total * (0.125 / LENGTH)

    for trial in range(2):
        arrived(recv1.at[trial], recv1_sem.at[trial])
        if trial == 0:
            arrived(fixed.at[pl.ds(0, SLOTS)], fix_sem.at[1])
            right = fixed[pl.ds(0, 64, stride=8), :]
            for rg, at in ((0, 0), (7, 127)):
                where = pl.ds(rg, 64, stride=8)
                recv1[0, where, :] = jnp.where(lane64 == at, right, recv1[0, where, :])
        transform(trial)
        exchange(
            send2.at[trial], recv2.at[trial], send2_sem.at[trial], recv2_sem.at[trial],
            block_of=class_at, order=far_first if trial else partners,
        )
    for trial in range(2):
        arrived(recv2.at[trial], recv2_sem.at[trial])
        finish(trial)
        share(trial)
    arrived(received.at[0], term_recv.at[0])
    collect(0)

    @pl.when(me < SLOTS - 1)
    def _():
        to_next.wait_send()

    @pl.when(me > 0)
    def _():
        to_last.wait_send()

    sent(fixes, fix_sem.at[0], 1)
    for trial in range(2):
        sent(send1.at[trial], send1_sem.at[trial])
        sent(send2.at[trial], send2_sem.at[trial])
    for copy, away in started:

        @pl.when(away)
        def _(copy=copy):
            copy.wait_send()

    arrived(received.at[1], term_recv.at[1])
    collect(1)


def on_device(series, filters, delays, phases):
    tables = [jnp.asarray(table) for table in make_tables()]
    whole = pl.BlockSpec(memory_space=pltpu.VMEM)
    anywhere = pl.BlockSpec(memory_space=pl.ANY)
    f32 = jnp.float32
    out = pl.pallas_call(
        kernel,
        out_shape=jax.ShapeDtypeStruct((2, 8, 128), f32),
        in_specs=[anywhere] * (4 + len(tables)),
        out_specs=whole,
        scratch_shapes=[
            pltpu.VMEM((2, 16), jnp.int32),
            pltpu.VMEM((2, 16), jnp.int32),
            pltpu.VMEM((TAPS, PHASES), f32),
            pltpu.VMEM((528, 128), f32),
            pltpu.VMEM((2, 8, 128), f32),
            pltpu.VMEM((512, 128), f32),
            pltpu.VMEM((512, 128), f32),
            pltpu.VMEM((32, 256), f32),
            pltpu.VMEM((8, 256, 128), jnp.bfloat16),
            pltpu.VMEM((8, 256, 128), jnp.bfloat16),
            pltpu.VMEM((2, 512, 128), f32),
            pltpu.VMEM((2, 512, 128), f32),
            pltpu.VMEM((2, 512, 128), f32),
            pltpu.VMEM((2, 512, 128), f32),
            pltpu.VMEM((2 * FREQS, 128), f32),
            pltpu.VMEM((2, FREQS, 128), f32),
            pltpu.VMEM((2, 64, 128), f32),
            pltpu.VMEM((2, 64, 128), f32),
            pltpu.VMEM((2, 40, 128), f32),
            pltpu.VMEM((2, TERM_ROWS, 128), f32),
        ]
        + [pltpu.VMEM(table.shape, table.dtype) for table in tables]
        + [
            pltpu.SemaphoreType.DMA((3,)),
            pltpu.SemaphoreType.DMA((len(tables),)),
            pltpu.SemaphoreType.DMA,
            pltpu.SemaphoreType.DMA((2,)),
            pltpu.SemaphoreType.DMA((2,)),
            pltpu.SemaphoreType.DMA((2,)),
            pltpu.SemaphoreType.DMA((2,)),
            pltpu.SemaphoreType.DMA((2,)),
            pltpu.SemaphoreType.DMA((2,)),
            pltpu.SemaphoreType.DMA((2,)),
            pltpu.SemaphoreType.DMA((2, 32)),
            pltpu.SemaphoreType.DMA((2,)),
        ],
        compiler_params=pltpu.CompilerParams(
            collective_id=0, has_side_effects=True
        ),
    )(series.reshape(512, 128), delays, phases, filters.T, *tables)
    return out.reshape(2, 1, 1024)


def solution(mesh):
    return jax.shard_map(
        on_device,
        mesh=mesh,
        in_specs=(P(("dm", "fft")), P(), P(None, "fft"), P(None, "fft")),
        out_specs=P("dm", "fft", None),
        check_vma=False,
    )
```

```python
import jax
import jax.numpy as jnp
import ml_dtypes
import numpy as np
from jax import lax
from jax.experimental import pallas as pl
from jax.experimental.pallas import tpu as pltpu
from jax.sharding import PartitionSpec as P

LENGTH = 4194304
SLOTS = 64
TAPS = 16
PHASES = 32
FIRST = 512
SECOND = 128
FREQS = 272
INVERSE = {1: 1, 3: 171, 5: 205, 7: 439}
BASES = {1: 0, 3: 16, 5: 32, 7: 48, 2: 64, 6: 96, 4: 128, 8: 144}
TERM_ROWS = 152
PAIRS = (
    6, 16, 3, 24, 18, 22, 2, 15, 5, 4, 21, 12, 28, 17, 31, 8,
    7, 9, 20, 19, 25, 11, 13, 26, 0, 30, 14, 10, 23, 29, 27, 1,
)


def split_table(table):
    table = np.asarray(table, np.float32)
    high = table.astype(ml_dtypes.bfloat16)
    low = (table - high.astype(np.float32)).astype(ml_dtypes.bfloat16)
    return high, low


def make_tables():
    turn = 2.0 * np.pi
    angle = turn / FIRST * (np.arange(FREQS)[:, None] * np.arange(FIRST)[None, :] % FIRST)
    first = np.concatenate([np.cos(angle), -np.sin(angle)], axis=0)
    h, rr, c_hi = np.meshgrid(np.arange(2), np.arange(2), np.arange(32), indexing="ij")
    second_index = (64 * rr + 2 * c_hi + h).reshape(-1)
    angle = turn / 65536 * (np.arange(FREQS)[:, None] * second_index[None, :] % 65536)
    mid = np.stack([np.cos(angle), -np.sin(angle)]).astype(np.float32)
    angle = turn / SECOND * (second_index[:, None] * np.arange(SECOND)[None, :] % SECOND)
    cos_part, sin_part = np.cos(angle), np.sin(angle)
    second = np.block([[cos_part, -sin_part], [sin_part, cos_part]])
    angle = turn / LENGTH * (np.arange(FREQS)[:, None] * np.arange(128)[None, :])
    col = np.stack([np.cos(angle), -np.sin(angle)]).astype(np.float32)
    angle = turn / 8192 * (np.arange(SLOTS)[:, None] * np.arange(SECOND)[None, :] % 8192)
    row = np.stack([np.cos(angle), -np.sin(angle)]).astype(np.float32)
    last = np.zeros((2, 8, 2, 4, SLOTS, 4, 2))
    special = np.zeros((2, 2, 8, SLOTS, 4, 2))
    q = np.arange(SLOTS)
    for sign in range(2):
        for p in range(8):
            actual = p if sign == 0 else -1 - p
            theta = turn / 64 * (q * actual % 64)
            for i in range(4):
                last[0, p, sign, i, :, i, 0] = np.cos(theta)
                last[0, p, sign, i, :, i, 1] = np.sin(theta)
                last[1, p, sign, i, :, i, 0] = -np.sin(theta)
                last[1, p, sign, i, :, i, 1] = np.cos(theta)
            theta = turn / 128 * (q * (2 * p + sign) % 128)
            special[0, sign, p, :, 0, sign] = np.cos(theta)
            special[1, sign, p, :, 0, sign] = -np.sin(theta)
    last = np.concatenate([last.reshape(128, 512), special.reshape(32, 512)], axis=0)
    return (*split_table(first), *split_table(second), *split_table(last), mid, col, row)


def split(x):
    high = x.astype(jnp.bfloat16)
    return high, (x - high.astype(jnp.float32)).astype(jnp.bfloat16)


def dot(a, b):
    return jnp.dot(a, b, preferred_element_type=jnp.float32)


def product(a_high, a_low, b_high, b_low):
    wide = dot(a_high, jnp.concatenate([b_high, b_low], 1))
    return wide[:, 0:128] + wide[:, 128:256] + dot(a_low, b_high)


def lanes_at(x, index):
    return jnp.take_along_axis(x, index, axis=1, mode="promise_in_bounds")


def iota(shape, axis):
    return lax.broadcasted_iota(jnp.int32, shape, axis)


def class_at(device):
    words = [sum(PAIRS[4 * n + b] << (8 * b) for b in range(4)) for n in range(8)]
    chip = device >> 1
    word = jnp.int32(words[0])
    for n in range(1, 8):
        word = jnp.where((chip >> 2) == n, jnp.int32(words[n]), word)
    pair = (word >> ((chip & 3) << 3)) & 31
    other = jnp.where(pair == 0, SLOTS // 2, SLOTS - pair)
    return jnp.where((device & 1) == 0, pair, other)


def column_of(values, own, second_trial):
    chosen = jnp.where(second_trial, values[1:2, :], values[0:1, :])
    return jnp.sum(jnp.where(own, chosen, 0.0), axis=1, keepdims=True)


def kernel(
    series, delays, phases, filters,
    first_high, first_low, second_high, second_low, last_high, last_low, mid, col, row,
    out,
    v_delays, v_phases, v_filters, ext, halos, fixes, fixed, responses, windows_high, windows_low, send1, recv1, send2, recv2, spectrum, turn,
    powers, rows_a, terms, received,
    v_first_high, v_first_low, v_second_high, v_second_low, v_last_high, v_last_low,
    v_mid, v_col, v_row,
    small_sem, table_sem, series_sem, halo_send, halo_recv, fix_sem,
    send1_sem, recv1_sem, send2_sem, recv2_sem, term_send, term_recv,
):
    me = lax.axis_index("fft")
    cls = class_at(me)
    f32 = jnp.float32
    mesh_id = pl.DeviceIdType.MESH

    barrier = pltpu.get_barrier_semaphore()

    def partner(act, dz, dy, dc):
        y, z = ((me >> 4) + dy) & 3, ((me >> 1) + dz) & 7
        act((y << 4) + (z << 1) + ((me & 1) ^ dc))

    def same_z(act):
        for dy in (2, 1, 3, 0):
            for dc in range(2):
                if dy or dc:
                    partner(act, 0, dy, dc)

    def partners(act):
        def block(step, carry):
            dy = (0x36 >> (step & 6)) & 3
            for dz in (3, 5, 4, 2, 6, 1, 7):
                partner(act, dz, dy, step & 1)
            return carry

        lax.fori_loop(0, 8, block, 0)
        same_z(act)

    def far_first(act):
        def ring(step, carry):
            dz = (0x7162534 >> (4 * step)) & 7
            for dy in (2, 1, 3, 0):
                for dc in range(2):
                    partner(act, dz, dy, dc)
            return carry

        lax.fori_loop(0, 7, ring, 0)
        same_z(act)

    def greet(to):
        pl.semaphore_signal(barrier, inc=1, device_id={"fft": to}, device_id_type=mesh_id)

    small = [
        pltpu.make_async_copy(source, target, small_sem.at[n])
        for n, (source, target) in enumerate(
            ((delays, v_delays), (phases, v_phases), (filters, v_filters))
        )
    ]
    for copy in small:
        copy.start()
    own_series = pltpu.make_async_copy(series, ext.at[pl.ds(8, 512)], series_sem)
    own_series.start()
    far_first(greet)
    tables = [
        pltpu.make_async_copy(source, target, table_sem.at[n])
        for n, (source, target) in enumerate(
            (
                (first_high, v_first_high), (first_low, v_first_low),
                (second_high, v_second_high), (second_low, v_second_low),
                (last_high, v_last_high), (last_low, v_last_low),
                (mid, v_mid), (col, v_col), (row, v_row),
            )
        )
    ]

    for copy in small:
        copy.wait()
    line = iota((32, 16), 0)
    own = iota((32, 16), 1) == 2 * (line >> 2) + (line & 1)
    second_trial = ((line >> 1) & 1) == 1
    delay = column_of(v_delays[...].astype(f32), own, second_trial)
    phase = column_of(v_phases[...].astype(f32), own, second_trial)
    taps = jnp.zeros((32, TAPS), f32)
    filter_rows = v_filters[...].T
    for number in range(PHASES):
        taps = jnp.where(phase == float(number), filter_rows[number : number + 1, :], taps)
    position = iota((32, 256), 1).astype(f32) - (delay + 56.0)
    response = jnp.zeros((32, 256), f32)
    for tap in range(TAPS):
        response = jnp.where(position == float(tap), taps[:, tap : tap + 1], response)
    responses[...] = response

    own_series.wait()
    ext[0:8, :] = jnp.zeros((8, 128), f32)
    ext[520:528, :] = jnp.zeros((8, 128), f32)

    lane64 = iota((64, 128), 1)

    def resample(trial, rg):
        if trial == 0:
            before = ext[pl.ds(64 * rg + 7, 64), :]
            here = ext[pl.ds(64 * rg + 8, 64), :]
            after = ext[pl.ds(64 * rg + 9, 64), :]
            left = pltpu.roll(jnp.where(lane64 < 64, here, before), 64, 1)
            right = pltpu.roll(jnp.where(lane64 < 64, after, here), 64, 1)
            window = jnp.concatenate(
                [jnp.concatenate([left, here], 0).T, jnp.concatenate([right, after], 0).T], 0
            )
            w_high, w_low = split(window)
            windows_high[rg], windows_low[rg] = w_high, w_low
        else:
            w_high, w_low = windows_high[rg], windows_low[rg]
        bands = []
        for rr in range(2):
            line = responses[pl.ds(4 * rg + 2 * trial + rr, 1), :]
            bands.append(
                pltpu.roll(jnp.broadcast_to(line, (64, 256)), 0, 1, stride=1, stride_axis=0)
            )
        b_high, b_low = split(jnp.concatenate(bands, 0))
        both = product(b_high, b_low, w_high, w_low)
        return jnp.where((lane64 & 32) == 0, both[0:64], both[64:128])

    def exchange(source, target, send_sem, recv_sem, rows=8, block_of=lambda device: device):
        mine = pl.ds(pl.multiple_of(8 * me, 8), rows)

        def block(device):
            return source.at[pl.ds(pl.multiple_of(8 * block_of(device), 8), rows)]

        def send(to):
            pltpu.make_async_remote_copy(
                src_ref=block(to), dst_ref=target.at[mine],
                send_sem=send_sem, recv_sem=recv_sem,
                device_id={"fft": to}, device_id_type=mesh_id,
            ).start()

        partners(send)
        pltpu.make_async_copy(block(me), target.at[mine], recv_sem).start()

    def arrived(target, sem):
        pltpu.make_async_copy(target, target, sem).wait()

    def sent(source, sem, rows=8):
        part = source.at[pl.ds(0, rows * (SLOTS - 1))]
        pltpu.make_async_copy(part, part, sem).wait()

    def inner(trial):
        def body(rg, carry):
            send1[trial, pl.ds(rg, 64, stride=8), :] = resample(trial, rg)
            return carry

        return body

    lax.fori_loop(0, 8, inner(0), 0)
    pl.semaphore_wait(barrier, SLOTS - 1)
    to_next = pltpu.make_async_remote_copy(
        src_ref=series.at[pl.ds(504, 8)], dst_ref=halos.at[0],
        send_sem=halo_send.at[0], recv_sem=halo_recv.at[0],
        device_id={"fft": (me + 1) & (SLOTS - 1)}, device_id_type=mesh_id,
    )
    to_last = pltpu.make_async_remote_copy(
        src_ref=series.at[pl.ds(0, 8)], dst_ref=halos.at[1],
        send_sem=halo_send.at[1], recv_sem=halo_recv.at[1],
        device_id={"fft": (me + SLOTS - 1) & (SLOTS - 1)}, device_id_type=mesh_id,
    )

    @pl.when(me < SLOTS - 1)
    def _():
        to_next.start()

    @pl.when(me > 0)
    def _():
        to_last.start()

    exchange(send1.at[0], recv1.at[0], send1_sem.at[0], recv1_sem.at[0])
    for copy in tables:
        copy.start()
    lax.fori_loop(1, 7, inner(1), 0)

    @pl.when(me > 0)
    def _():
        to_next.wait_recv()
        ext[0:8, :] = halos[0]

    @pl.when(me < SLOTS - 1)
    def _():
        to_last.wait_recv()
        ext[520:528, :] = halos[1]

    def fix(end, held):
        return jnp.where(lane64 >= 64 * end, resample(0, 7 * end), held)

    fixes[pl.ds(0, 64, stride=8), :] = lax.fori_loop(0, 2, fix, jnp.zeros((64, 128), f32))
    exchange(fixes, fixed, fix_sem.at[0], fix_sem.at[1], 1)
    lax.fori_loop(0, 2, lambda end, carry: inner(1)(7 * end, carry), 0)
    exchange(send1.at[1], recv1.at[1], send1_sem.at[1], recv1_sem.at[1])

    for copy in tables:
        copy.wait()
    me_lane = iota((FREQS, 128), 1) == me
    col_cos = jnp.sum(jnp.where(me_lane, v_col[0], 0.0), axis=1, keepdims=True)
    col_sin = jnp.sum(jnp.where(me_lane, v_col[1], 0.0), axis=1, keepdims=True)
    row_cos = v_row[0, pl.ds(me, 1), :]
    row_sin = v_row[1, pl.ds(me, 1), :]
    turn[0] = col_cos * row_cos - col_sin * row_sin
    turn[1] = col_cos * row_sin + col_sin * row_cos
    lane1 = iota((1, 128), 1)
    lane8, sub8 = iota((8, 128), 1), iota((8, 128), 0)

    def transform(trial):
        d_high, d_low = split(recv1[trial])
        spectrum[...] = product(v_first_high[...], v_first_low[...], d_high, d_low)
        real, imaginary = spectrum[0:FREQS, :], spectrum[FREQS : 2 * FREQS, :]
        mid_cos, mid_sin = v_mid[0], v_mid[1]
        turned = jnp.concatenate(
            [real * mid_cos - imaginary * mid_sin, real * mid_sin + imaginary * mid_cos], 1
        )
        t_high, t_low = split(turned)
        s_high = v_second_high[...]
        result = dot(t_high, s_high) + dot(t_low, s_high) + dot(t_high, v_second_low[...])
        real, imaginary = result[:, 0:128], result[:, 128:256]
        turn_cos, turn_sin = turn[0], turn[1]
        parts = (
            real * turn_cos - imaginary * turn_sin,
            real * turn_sin + imaginary * turn_cos,
        )
        middle = pltpu.roll(real[0:1], 64, 1)
        for c in range(2):
            for i in range(4):
                send2[trial, pl.ds(2 * i + c, 64, stride=8), :] = parts[c][64 * i : 64 * i + 64]
            packed = jnp.where(lane1 < 64, parts[c][0:1], pltpu.roll(parts[c][256:257], 64, 1))
            if c == 1:
                packed = jnp.where(lane1 == 0, middle, packed)
            send2[trial, c : c + 1, :] = packed

    def finish(trial):
        r_high, r_low = split(recv2[trial])
        final = product(v_last_high[...], v_last_low[...], r_high, r_low)
        power = powers.at[trial]
        power[...] = final[0:64] ** 2 + final[64:128] ** 2
        special = final[128:144] ** 2 + final[144:160] ** 2

        @pl.when(cls == 0)
        def _():
            for sign in range(2):
                where = pl.ds(4 * sign, 8, stride=8)
                power[where, :] = jnp.where(
                    lane8 == 0, special[8 * sign : 8 * sign + 8], power[where, :]
                )
            for p in range(8):
                x = power[8 * p : 8 * p + 8, :]
                one = lanes_at(
                    pltpu.roll(x, 7, 0), jnp.where(sub8 == 7, lane8 + 64, 127 - lane8) & 127
                )
                two = lanes_at(
                    jnp.where(sub8 == 0, pltpu.roll(x, 4, 0), pltpu.roll(x, 3, 0)),
                    jnp.where(sub8 == 0, (128 - lane8) & 63, (191 - lane8) & 127),
                )
                head = jnp.where((sub8 == 0) & (lane8 >= 64), two, x)
                tail = jnp.where((sub8 == 7) & (lane8 >= 64), two, one)
                power[8 * p : 8 * p + 8, :] = jnp.where(sub8 < 4, head, tail)

        @pl.when(cls != 0)
        def _():
            for p in range(8):
                x = power[8 * p : 8 * p + 8, :]
                power[8 * p : 8 * p + 8, :] = jnp.where(sub8 < 4, x, lanes_at(x, 127 - lane8))

        for n in range(8):
            rows_a[trial, 8 * n : 8 * n + 8, :] = power[pl.ds(n, 8, stride=8), :]

    def residue(sign):
        return cls if sign == 0 else (SLOTS - cls) & (SLOTS - 1)

    class_of = jnp.where(sub8 < 4, cls, (SLOTS - cls) & (SLOTS - 1)) + 64 * jnp.where(
        sub8 < 4, sub8, 11 - sub8
    )

    def select(trial, m, odd, shift, half):
        k1 = (INVERSE[odd] * (class_of >> shift)) & ((FIRST >> shift) - 1)
        index = ((m * k1) >> 9) + odd * (128 * half + lane8)
        total = jnp.zeros((8, 128), f32)
        for p in range(odd * half, odd * half + odd):
            total = jnp.where(
                (index >> 7) == p,
                lanes_at(powers[trial, 8 * p : 8 * p + 8, :], index & 127),
                total,
            )
        return total

    started = []

    def share(trial):
        power, by_row, term = powers.at[trial], rows_a.at[trial], terms.at[trial]
        number = [0]

        def give(source, start, m, sign, rows, to, condition):
            base = BASES[m] + (0 if m == 8 else rows * sign)
            from_ref = source.at[pl.ds(start, rows)]
            to_ref = received.at[trial, pl.ds(base, rows)]
            copy = pltpu.make_async_remote_copy(
                src_ref=from_ref, dst_ref=to_ref,
                send_sem=term_send.at[trial, number[0]], recv_sem=term_recv.at[trial],
                device_id={"fft": to}, device_id_type=mesh_id,
            )
            number[0] += 1
            away = condition & (to != me)

            @pl.when(away)
            def _():
                copy.start()

            @pl.when(condition & (to == me))
            def _():
                pltpu.make_async_copy(from_ref, to_ref, term_recv.at[trial]).start()

            started.append((copy, away))

        always, even = me >= 0, (cls & 1) == 0
        for sign in range(2):
            rest = residue(sign)
            give(power, 0, 1, sign, 8, rest, always)
            for v in range(2):
                give(power, 0, 2, sign, 16, ((rest >> 1) + 32 * v) & 63, even)
            for i in range(4):
                place = i if sign == 0 else 7 - i
                at = 32 * sign + 8 * i
                give(by_row, at, 4, sign, 8, ((rest >> 2) + 16 * place) & 63, (cls & 3) == 0)
                give(by_row, at, 8, sign, 8, ((rest >> 3) + 8 * place) & 63, (cls & 7) == 0)
        for n, m in enumerate((3, 5, 7)):
            term[8 * n : 8 * n + 8, :] = select(trial, m, m, 0, 0)
            for sign in range(2):
                give(term, 8 * n, m, sign, 8, (INVERSE[m] * residue(sign)) & 63, always)
        for half in range(2):
            term[24 + 8 * half : 32 + 8 * half, :] = select(trial, 6, 3, 1, half)
        for sign in range(2):
            for v in range(2):
                to = (INVERSE[3] * ((residue(sign) >> 1) + 32 * v)) & 63
                give(term, 24, 6, sign, 16, to, even)

    def source_row(m, v, rows):
        place = (((m * me) >> 6) + m * v) & 7
        sign = place >> 2
        slot = jnp.where(sign == 1, 7 - place, place)
        return BASES[m] + (rows + 4) * sign + slot

    def collect(trial):
        def row_at(index):
            return received[trial, pl.ds(index, 1), :]

        total = received[trial, pl.ds(BASES[8], 8), :]
        for v in range(2):
            base = BASES[4] + 8 * v
            values = jnp.broadcast_to(row_at(base), (8, 128))
            for p in range(1, 4):
                values = jnp.where((sub8 >> 1) == p, row_at(base + p), values)
            values = lanes_at(values, 64 * (sub8 & 1) + (lane8 >> 1))
            total = total + jnp.where((lane8 & 1) == v, values, 0.0)
        for v in range(4):
            at2, at6 = source_row(2, v, 16), source_row(6, v, 16)
            low = row_at(at2) + row_at(at6)
            high = row_at(at2 + 8) + row_at(at6 + 8)
            values = jnp.where((sub8 >> 2) == 0, low, high)
            values = lanes_at(values, 32 * (sub8 & 3) + (lane8 >> 2))
            total = total + jnp.where((lane8 & 3) == v, values, 0.0)
        for v in range(8):
            values = row_at(source_row(1, v, 8))
            for m in (3, 5, 7):
                values = values + row_at(source_row(m, v, 8))
            values = lanes_at(jnp.broadcast_to(values, (8, 128)), 16 * sub8 + (lane8 >> 3))
            total = total + jnp.where((lane8 & 7) == v, values, 0.0)
        out[trial] = total * (0.125 / LENGTH)

    for trial in range(2):
        arrived(recv1.at[trial], recv1_sem.at[trial])
        if trial == 0:
            arrived(fixed.at[pl.ds(0, SLOTS)], fix_sem.at[1])
            right = fixed[pl.ds(0, 64, stride=8), :]
            for rg, at in ((0, 0), (7, 127)):
                where = pl.ds(rg, 64, stride=8)
                recv1[0, where, :] = jnp.where(lane64 == at, right, recv1[0, where, :])
        transform(trial)
        exchange(
            send2.at[trial], recv2.at[trial], send2_sem.at[trial], recv2_sem.at[trial],
            block_of=class_at,
        )
    for trial in range(2):
        arrived(recv2.at[trial], recv2_sem.at[trial])
        finish(trial)
        share(trial)
    arrived(received.at[0], term_recv.at[0])
    collect(0)

    @pl.when(me < SLOTS - 1)
    def _():
        to_next.wait_send()

    @pl.when(me > 0)
    def _():
        to_last.wait_send()

    sent(fixes, fix_sem.at[0], 1)
    for trial in range(2):
        sent(send1.at[trial], send1_sem.at[trial])
        sent(send2.at[trial], send2_sem.at[trial])
    for copy, away in started:

        @pl.when(away)
        def _(copy=copy):
            copy.wait_send()

    arrived(received.at[1], term_recv.at[1])
    collect(1)


def on_device(series, filters, delays, phases):
    tables = [jnp.asarray(table) for table in make_tables()]
    whole = pl.BlockSpec(memory_space=pltpu.VMEM)
    anywhere = pl.BlockSpec(memory_space=pl.ANY)
    f32 = jnp.float32
    out = pl.pallas_call(
        kernel,
        out_shape=jax.ShapeDtypeStruct((2, 8, 128), f32),
        in_specs=[anywhere] * (4 + len(tables)),
        out_specs=whole,
        scratch_shapes=[
            pltpu.VMEM((2, 16), jnp.int32),
            pltpu.VMEM((2, 16), jnp.int32),
            pltpu.VMEM((TAPS, PHASES), f32),
            pltpu.VMEM((528, 128), f32),
            pltpu.VMEM((2, 8, 128), f32),
            pltpu.VMEM((512, 128), f32),
            pltpu.VMEM((512, 128), f32),
            pltpu.VMEM((32, 256), f32),
            pltpu.VMEM((8, 256, 128), jnp.bfloat16),
            pltpu.VMEM((8, 256, 128), jnp.bfloat16),
            pltpu.VMEM((2, 512, 128), f32),
            pltpu.VMEM((2, 512, 128), f32),
            pltpu.VMEM((2, 512, 128), f32),
            pltpu.VMEM((2, 512, 128), f32),
            pltpu.VMEM((2 * FREQS, 128), f32),
            pltpu.VMEM((2, FREQS, 128), f32),
            pltpu.VMEM((2, 64, 128), f32),
            pltpu.VMEM((2, 64, 128), f32),
            pltpu.VMEM((2, 40, 128), f32),
            pltpu.VMEM((2, TERM_ROWS, 128), f32),
        ]
        + [pltpu.VMEM(table.shape, table.dtype) for table in tables]
        + [
            pltpu.SemaphoreType.DMA((3,)),
            pltpu.SemaphoreType.DMA((len(tables),)),
            pltpu.SemaphoreType.DMA,
            pltpu.SemaphoreType.DMA((2,)),
            pltpu.SemaphoreType.DMA((2,)),
            pltpu.SemaphoreType.DMA((2,)),
            pltpu.SemaphoreType.DMA((2,)),
            pltpu.SemaphoreType.DMA((2,)),
            pltpu.SemaphoreType.DMA((2,)),
            pltpu.SemaphoreType.DMA((2,)),
            pltpu.SemaphoreType.DMA((2, 32)),
            pltpu.SemaphoreType.DMA((2,)),
        ],
        compiler_params=pltpu.CompilerParams(
            collective_id=0, has_side_effects=True
        ),
    )(series.reshape(512, 128), delays, phases, filters.T, *tables)
    return out.reshape(2, 1, 1024)


def solution(mesh):
    return jax.shard_map(
        on_device,
        mesh=mesh,
        in_specs=(P(("dm", "fft")), P(), P(None, "fft"), P(None, "fft")),
        out_specs=P("dm", "fft", None),
        check_vma=False,
    )
```
